32 devices in a mesh: dp: 8 (over z, x), seq: 4 (over y, core).
Axes of the slice: x: 2, y: 2, z: 4, core: 2. Of those that a mesh axis runs over, the one named last changes fastest.
Arguments:
- tokens: bfloat16 [8192, 512], P(('dp', 'seq')), may hold values from -6 to 6
- memory: bfloat16 [8192, 512], P(('dp', 'seq')), may hold values from -6 to 6
- cotangent: bfloat16 [8192, 512], P(('dp', 'seq')), may hold values from -6 to 6
- arrival_order: int32 [8192], replicated, may hold values from 0 to 8191, as said below
- lengths: int32 [64], replicated, may hold values from 1 to 512, as said below
- real_flag: int32 [64], replicated, may hold values from 0 to 1, as said below
- self_proj: bfloat16 [3, 512, 512], replicated, may hold values from -0.25 to 0.25
- cross_proj: bfloat16 [3, 512, 512], replicated, may hold values from -0.25 to 0.25
- mixers: bfloat16 [2, 512, 512], replicated, may hold values from -1 to 1
- expander: bfloat16 [512, 2048], replicated, may hold values from -0.25 to 0.25
- shrinker: bfloat16 [2048, 512], replicated, may hold values from -0.125 to 0.125
- norm_gains: float32 [3, 512], replicated, may hold values from 0.5 to 1.5
- norm_shifts: float32 [3, 512], replicated, may hold values from -0.5 to 0.5
Outputs:
- layer_out: bfloat16 [8192, 512], P(('dp', 'seq'))
- token_grad: bfloat16 [8192, 512], P(('dp', 'seq'))
- memory_grad: bfloat16 [8192, 512], P(('dp', 'seq'))
- self_grad: float32 [3, 512, 512], replicated
- cross_grad: float32 [3, 512, 512], replicated
- mixers_grad: float32 [2, 512, 512], replicated
- expander_grad: float32 [512, 2048], replicated
- shrinker_grad: float32 [2048, 512], replicated
- gains_grad: float32 [3, 512], replicated
- shifts_grad: float32 [3, 512], replicated
The draws below stay inside these ranges and needn't reach their ends.
Inputs may be any that keep to these rules, and one draw needn't show every extreme that they name: `arrival_order`: A permutation. Sentences stand in id order, token t of sentence j being position t - (sum of the lengths of sentences before j). The rows of one device hold tokens of sentences of exactly 4 bucket groups, 64 rows for each of them; the devices with one seq index together hold exactly 256 tokens of each bucket group. `lengths`: bucket group g holds the 8 sentences g * 8 to (g + 1) * 8 - 1; they have 4 * 256 tokens together, and one of them has 512. `real_flag`: A group's sentence of 512 tokens is real.
All inputs are finite; a program needn't handle non-finite values.
Results may differ from the reference program's by a relative error of at most 0.025.
Values may be sent and summed in bfloat16 or wider, within the bound.
A program may use at most 128 MiB of HBM per device.

```python
import jax
import jax.numpy as jnp
from jax import lax

D = 512
FF = 2048
HEADS = 8
HEAD = 64
TOK_DEV = 256
LMAX = 512
SENT_GROUP = 8
CAP = 64
SENTS = 64
TOKENS = 8192
N_DP = 8
N_SEQ = 4


def shared_plan(key):
    groups = N_DP
    lanes = N_SEQ
    per_device = TOK_DEV
    per_group = SENT_GROUP
    total = lanes * per_device
    rest = total - LMAX
    base = rest // (per_group - 1)
    half = base // 2
    couples = (per_group - 2) // 2
    streams = jax.random.split(key, 8)
    offset_draw = jax.random.randint(streams[0], (groups, couples), -half, half + 1)
    others = jnp.concatenate([base + offset_draw, base - offset_draw, jnp.full((groups, 1), rest - 2 * couples * base, jnp.int32)], axis=1)
    local = jnp.concatenate([jnp.full((groups, 1), LMAX, jnp.int32), others], axis=1).astype(jnp.int32)
    genuine = jnp.concatenate([jnp.ones((groups, 1), jnp.int32), (jax.random.randint(streams[1], (groups, per_group - 1), 0, 10) < 3).astype(jnp.int32)], axis=1)
    shuffle = jax.random.permutation(streams[2], jnp.broadcast_to(jnp.arange(per_group, dtype=jnp.int32), (groups, per_group)), axis=1, independent=True)
    local = jnp.take_along_axis(local, shuffle, axis=1)
    genuine = jnp.take_along_axis(genuine, shuffle, axis=1)
    count = groups * per_group
    identity = jnp.arange(count, dtype=jnp.int32).reshape(groups, per_group)
    lengths = local.reshape(count).astype(jnp.int32)
    flags = genuine.reshape(count).astype(jnp.int32)
    ends = jnp.cumsum(lengths).astype(jnp.int32)
    starts = ends - lengths
    offsets = jnp.cumsum(local, axis=1) - local
    spots = jnp.arange(total, dtype=jnp.int32)
    which = jnp.sum((offsets[:, None, :] <= spots[None, :, None]).astype(jnp.int32), axis=-1) - 1
    sentence_ids = jnp.take_along_axis(identity, which, axis=1)
    canonical = starts[sentence_ids] + spots[None, :] - jnp.take_along_axis(offsets, which, axis=1)
    canonical = canonical.reshape(groups, per_device, lanes)
    first_perm = jax.vmap(lambda sub: jax.random.permutation(sub, groups))(jax.random.split(streams[4], lanes)).astype(jnp.int32)
    second_perm = jax.vmap(lambda sub: jax.random.permutation(sub, groups))(jax.random.split(streams[5], lanes)).astype(jnp.int32)
    reach = (first_perm[:, None, :] - second_perm[:, :, None]) % groups < groups // 2
    labels = jnp.arange(groups, dtype=jnp.int32)
    chosen = jnp.argsort(jnp.where(reach, labels, labels + groups), axis=-1)[..., :groups // 2].astype(jnp.int32)
    listing = jnp.repeat(chosen, CAP, axis=-1)
    destination = jax.random.permutation(streams[6], listing, axis=2, independent=True)
    hits = destination[..., None] == labels
    slot = jnp.sum(jnp.where(hits, jnp.cumsum(hits.astype(jnp.int32), axis=2), 0), axis=-1) - 1
    reach_count = reach.astype(jnp.int32)
    before = jnp.cumsum(reach_count, axis=1) - reach_count
    arrival = jnp.take_along_axis(before, destination, axis=2) * CAP + slot
    mixing = jax.random.permutation(streams[7], jnp.broadcast_to(jnp.arange(per_device, dtype=jnp.int32), (lanes, groups, per_device)), axis=2, independent=True)
    lane_index = jnp.arange(lanes, dtype=jnp.int32)[:, None, None]
    spot_index = mixing[lane_index, destination, arrival]
    token = canonical[destination, spot_index, lane_index]
    order = jnp.transpose(token, (1, 0, 2)).reshape(-1).astype(jnp.int32)
    return (order, lengths, flags)


def draw_arrival_order(key, part):
    shared = shared_plan(key)
    return shared[0]


def draw_lengths(key, part):
    shared = shared_plan(key)
    return shared[1]


def draw_real_flag(key, part):
    shared = shared_plan(key)
    return shared[2]


def level_of(rng, extent, cuts, least, top_value):
    def one(dim, blocks):
        draws = jax.random.uniform(jax.random.fold_in(jax.random.fold_in(rng, 6), dim), (blocks,), jnp.float32, least / len(cuts), top_value / len(cuts))
        return jnp.repeat(jnp.exp(draws), extent[dim] // blocks).reshape((-1,) + (1,) * (len(extent) - dim - 1))

    loudness = one(*cuts[0])
    for cut in cuts[1:]:
        loudness = loudness * one(*cut)
    return loudness


def normal_values(key, shape, deviation, limit, shards=(), kind=jnp.bfloat16):
    result = jax.random.normal(key, shape, jnp.float32) * deviation
    if len(shards) > 0:
        result = level_of(key, shape, shards, -0.22, 0.18) * result
    return jnp.clip(result, min=-limit, max=limit).astype(kind)


def setup_inputs(seed: int = 0) -> dict:
    arg_keys = jax.random.split(jax.random.key(seed), 14)
    return {
        "tokens": normal_values(arg_keys[0], (TOKENS, D), 1.0, 6.0, ((0, 32),)),
        "memory": normal_values(arg_keys[1], (TOKENS, D), 1.0, 6.0, ((0, 32),)),
        "cotangent": normal_values(arg_keys[2], (TOKENS, D), 1.0, 6.0, ((0, 32),)),
        "arrival_order": draw_arrival_order(jax.random.fold_in(arg_keys[13], 71), 0),
        "lengths": draw_lengths(jax.random.fold_in(arg_keys[13], 71), 0),
        "real_flag": draw_real_flag(jax.random.fold_in(arg_keys[13], 71), 0),
        "self_proj": normal_values(arg_keys[6], (3, D, D), D ** -0.5, 0.25),
        "cross_proj": normal_values(arg_keys[7], (3, D, D), D ** -0.5, 0.25),
        "mixers": normal_values(arg_keys[8], (2, D, D), (D // 16) ** -0.5, 1.0),
        "expander": normal_values(arg_keys[9], (D, FF), D ** -0.5, 0.25),
        "shrinker": normal_values(arg_keys[10], (FF, D), FF ** -0.5, 0.125),
        "norm_gains": jnp.clip(1.0 + 0.1 * jax.random.normal(arg_keys[11], (3, D), jnp.float32), 0.5, 1.5),
        "norm_shifts": jnp.clip(jax.random.uniform(arg_keys[12], (3, D), jnp.float32, -0.5, 0.5), -0.5, 0.5),
    }


@jax.custom_vjp
def low(v):
    return lax.optimization_barrier(v.astype(jnp.bfloat16)).astype(jnp.float32)

@jax.custom_vjp
def low_back(v):
    return v

def low_keep(v):
    return (low(v), None)

def low_pass(kept, grad):
    return (grad,)

def back_keep(v):
    return (v, None)

def back_low(kept, grad):
    return (low(grad),)
low.defvjp(low_keep, low_pass)
low_back.defvjp(back_keep, back_low)
synth_weight = 0.4
score_fill = -1e+30
epsilon = 1e-05
highest = lax.Precision.HIGHEST

def rounded_both(values):
    return low(low_back(values))

def normalize(values, gain, shift):
    center = values - lax.optimization_barrier(jnp.mean(values, axis=-1, keepdims=True))
    spread = lax.optimization_barrier(jnp.mean(center * center, axis=-1, keepdims=True))
    return center * lax.rsqrt(spread + epsilon) * gain + shift

def reference(tokens, memory, cotangent, arrival_order, lengths, real_flag, self_proj, cross_proj, mixers, expander, shrinker, norm_gains, norm_shifts):
    ends = jnp.cumsum(lengths).astype(jnp.int32)
    starts = (ends - lengths).astype(jnp.int32)
    sentence = jnp.searchsorted(ends, arrival_order, side='right').astype(jnp.int32)
    position = (arrival_order - starts[sentence]).astype(jnp.int32)
    inverse = jnp.zeros((TOKENS,), jnp.int32).at[arrival_order].set(jnp.arange(TOKENS, dtype=jnp.int32))
    places = jnp.arange(LMAX, dtype=jnp.int32)
    present = places[None, :] < lengths[:, None]
    canonical = jnp.where(present, starts[:, None] + places[None, :], 0).astype(jnp.int32)
    fetch = inverse[canonical]
    per_block = 4
    blocks = SENTS // per_block
    fetch_blocks = fetch.reshape(blocks, per_block, LMAX)
    present_blocks = present.reshape(blocks, per_block, LMAX)
    weight = jnp.where(real_flag[sentence] > 0, 1.0, synth_weight).astype(jnp.float32)
    weighted_cot = cotangent.astype(jnp.float32) * weight[:, None]
    scale = HEAD ** (-0.5)
    causal_table = places[None, :] <= places[:, None]

    def attention(queries, keys_rows, values_rows, causal):

        def block(carry, items):
            rows_index, live = items
            query_block = queries[rows_index].reshape(per_block, LMAX, HEADS, HEAD)
            key_block = keys_rows[rows_index].reshape(per_block, LMAX, HEADS, HEAD)
            value_block = values_rows[rows_index].reshape(per_block, LMAX, HEADS, HEAD)
            raw = jnp.einsum('bqhd,bkhd->bhqk', query_block, key_block, precision=highest) * scale
            scores = low_back(raw)
            allowed = live[:, None, None, :]
            if causal:
                allowed = allowed & causal_table[None, None, :, :]
            scores = jnp.where(allowed, scores, score_fill)
            probs = low(jax.nn.softmax(scores, axis=-1))
            mixed = jnp.einsum('bhqk,bkhd->bqhd', probs, value_block, precision=highest)
            return (carry, mixed.reshape(per_block, LMAX, HEADS * HEAD))
        _, stacked = lax.scan(jax.checkpoint(block), None, (fetch_blocks, present_blocks))
        stacked = stacked.reshape(SENTS, LMAX, HEADS * HEAD)
        return rounded_both(stacked[sentence, position])

    def forward(inputs, memory_rows, self_weights, cross_weights, mixer_weights, expand_weights, shrink_weights, gains, shifts):
        queries = rounded_both(jnp.dot(inputs, self_weights[0], precision=highest))
        keys_rows = rounded_both(jnp.dot(inputs, self_weights[1], precision=highest))
        values_rows = rounded_both(jnp.dot(inputs, self_weights[2], precision=highest))
        self_mixed = attention(queries, keys_rows, values_rows, True)
        first = normalize(inputs + low_back(jnp.dot(self_mixed, mixer_weights[0], precision=highest)), gains[0], shifts[0])
        first_low = low(first)
        cross_queries = rounded_both(jnp.dot(first_low, cross_weights[0], precision=highest))
        cross_keys = rounded_both(jnp.dot(memory_rows, cross_weights[1], precision=highest))
        cross_values = rounded_both(jnp.dot(memory_rows, cross_weights[2], precision=highest))
        cross_mixed = attention(cross_queries, cross_keys, cross_values, False)
        second = normalize(first + low_back(jnp.dot(cross_mixed, mixer_weights[1], precision=highest)), gains[1], shifts[1])
        second_low = low(second)
        pre = low_back(jnp.dot(second_low, expand_weights, precision=highest))
        hidden = low(jax.nn.silu(pre))
        return normalize(second + low_back(jnp.dot(hidden, shrink_weights, precision=highest)), gains[2], shifts[2])
    primal, pullback = jax.vjp(forward, tokens.astype(jnp.float32), memory.astype(jnp.float32), self_proj.astype(jnp.float32), cross_proj.astype(jnp.float32), mixers.astype(jnp.float32), expander.astype(jnp.float32), shrinker.astype(jnp.float32), norm_gains.astype(jnp.float32), norm_shifts.astype(jnp.float32))
    grads = pullback(weighted_cot)
    return (primal.astype(jnp.bfloat16), grads[0].astype(jnp.bfloat16), grads[1].astype(jnp.bfloat16), grads[2], grads[3], grads[4], grads[5], grads[6], grads[7], grads[8])
```

```python
import functools

import jax
import jax.numpy as jnp
from jax import lax
from jax.experimental import pallas as pl
from jax.experimental.pallas import tpu as pltpu
from jax.sharding import PartitionSpec as P

HEAD = 64
PAIR = 2 * HEAD
MESH = pl.DeviceIdType.MESH
F32 = jnp.float32
BF16 = jnp.bfloat16
EPSILON = 1e-05
SYNTH_WEIGHT = 0.4
SCORE_FILL = -1e30
LAYER_VMEM = 55 * 1024 * 1024
FINISH_VMEM = 24 * 1024 * 1024

(
    P00, P01, P02, P03, P10, P11, P12, P13, N0, N1, X1, X2,
    OUT, RET0, RET1, NORM, SHR0, EXP0, SHR1, EXP1, CROSS_Q, CROSS_KV,
    SELF_Q, SELF_KV,
) = range(24)
(
    START, PACK1, PACK2, PLACE, SLOTS, LANE0, LANE1, LANE2, LANE3, BIAS,
    OWN0, Q0, NEAR0, FAR0, DIAG0, SATT0, SATT1, LN0, CQ, OWN1,
    KV1, NEAR1, FAR1, DIAG1, CATT0, CATT1, LN1, FFN0, FFN1, LN2,
    COT, FB0, FB1, FB2, FB3, LN1B, CROSS_B0, CROSS_B1, CROSS_ROW, CROSS_SQ,
    CROSS_SK, CROSS_SV, LN0B, MIX0, SELF_B0, SELF_B1, SELF_ROW, SELF_SQ, SELF_SK, SELF_SV,
) = range(50)
PLAN = {
    LANE0: (P00,),
    LANE1: (P01,),
    BIAS: (P02, X1, P00, P03),
    Q0: (P01, P02, N0, P10, P01),
    NEAR0: (P03,),
    FAR0: (P11, P12, P03),
    SATT1: (P13,),
    OWN1: (X2, P10),
    KV1: (P12, P11, P13, N1),
    FAR1: (P11, P13),
    LN1B: (SHR0,),
    CROSS_B1: (EXP1,),
    CROSS_SQ: (SHR1, EXP0),
    LN0B: (EXP1,),
    MIX0: (RET1, CROSS_Q, CROSS_KV, SHR0),
    SELF_B1: (RET1,),
    SELF_ROW: (EXP0,),
    SELF_SQ: (CROSS_KV, CROSS_Q),
    SELF_SK: (SHR0,),
    SELF_SV: (
        SELF_Q, EXP0, SHR0, CROSS_Q, SELF_KV, EXP1, EXP0, RET0,
        SHR0, SELF_Q, CROSS_KV, CROSS_Q, SHR0, SELF_KV, EXP0, EXP1,
        SELF_Q, SHR1, CROSS_Q, EXP0, CROSS_KV, EXP1, SELF_KV, SHR0,
        SELF_Q, CROSS_Q, SHR1, NORM, SELF_KV, CROSS_KV, EXP1, SELF_Q,
        EXP0, SHR1, CROSS_Q, SELF_Q, SHR0, RET1, SELF_KV, EXP1,
        CROSS_KV, SHR1, EXP0, NORM, SELF_KV, CROSS_KV, SELF_Q, SHR1,
        CROSS_Q, SELF_KV, RET0, EXP1, CROSS_Q, SHR1, EXP0, CROSS_KV,
        SELF_Q, EXP1, SHR0, NORM, OUT, SELF_KV, SELF_Q, SHR1,
        NORM, CROSS_KV, SELF_KV, RET0, NORM, SHR1,
    ),
}
ORDERS = {
    SHR0: (0, 2, 1, 3, 4),
    EXP0: (0, 1, 2, 3, 4),
    SHR1: (0, 2, 1, 3, 4),
    EXP1: (0, 1, 3, 2, 4),
    CROSS_Q: (0, 2, 1, 3, 4),
    CROSS_KV: (0, 3, 2, 1, 4),
    SELF_Q: (0, 2, 3, 1, 4),
    SELF_KV: (0, 1, 2, 3, 4),
}


def contract(a, b, left, right):
    return lax.dot_general(a, b, (((left,), (right,)), ((), ())), preferred_element_type=F32)


def nn(a, b):
    return contract(a, b, 1, 0)


def nt(a, b):
    return contract(a, b, 1, 1)


def tn(a, b):
    return contract(a, b, 0, 0)


def block(index, size):
    if isinstance(index, int):
        return pl.ds(index * size, size)
    return pl.ds(pl.multiple_of(index * size, size), size)


def rows_at(offset, size):
    if isinstance(offset, int):
        return pl.ds(offset, size)
    return pl.ds(pl.multiple_of(offset, 16), size)


def loop(count, step):
    def body(index, carry):
        step(index)
        return carry

    lax.fori_loop(0, count, body, 0)


def iota(shape, axis):
    return lax.broadcasted_iota(jnp.int32, shape, axis)


class Sizes:
    def __init__(self, n_dp, n_seq, rows, width, ff, sentences):
        self.n_dp, self.n_seq, self.rows, self.width, self.ff = n_dp, n_seq, rows, width, ff
        self.cap = 2 * rows // n_dp
        self.group_sents = sentences // n_dp
        self.parts = max(1, 16 // self.cap)
        self.prow = self.cap * self.parts
        self.pcol = width // self.parts
        self.slots = n_dp * self.prow
        self.passes = self.parts == 1
        self.lanes_packed = n_seq if self.passes else 1
        self.keys = n_seq * rows
        self.pairs = width // PAIR
        self.ff_blocks = ff // width
        lane_bits = [("seq", b) for b in range(n_seq.bit_length() - 1)]
        dp_bits = [("dp", b) for b in range(n_dp.bit_length() - 1)]
        self.planned = (n_dp, n_seq) == (8, 4)
        links = (("seq", 0), ("dp", 0), ("seq", 1), ("dp", 1), ("dp", 2))
        self.order_a = lane_bits[:1] + dp_bits[:2] + lane_bits[1:] + dp_bits[2:]
        self.order_b = lane_bits + dp_bits[1:2] + dp_bits[:1] + dp_bits[2:]
        self.stages = len(self.order_a)
        w = width
        self.units, row = {}, 0
        half = self.ff_blocks // 2
        names = [(name, half) for name in (SHR0, EXP0, SHR1, EXP1)]
        names += [(name, 2) for name in (CROSS_Q, CROSS_KV, SELF_Q, SELF_KV)]
        for name, blocks in names:
            order = (self.order_a, self.order_b)[len(self.units) % 2]
            if self.planned:
                order = [links[c] for c in ORDERS[name]]
            self.units[name] = (len(self.units), row, blocks * w, 0, w, order)
            row += blocks * w
        self.sum_rows = row
        self.land, spot = {}, 0
        for name, (_, _, count, _, _, _) in self.units.items():
            self.land[name] = spot
            n = count
            for s in range(self.stages):
                n = n // 2 if self.halves(n, s) else n
                spot += n
        self.land_rows = spot

    def halves(self, count, stage):
        return count % 32 == 0 and stage < self.stages - 1


def scratch_list(z):
    w, r, k = z.width, z.rows, z.keys
    v = pltpu.VMEM
    dma = pltpu.SemaphoreType.DMA
    n_units = len(z.units)
    if z.passes:
        extra = {"passed": v((2, 3, z.slots, z.pcol), BF16)}
    else:
        extra = {"hidden": v((z.ff_blocks, r, w), BF16)}
    return extra | {
        "row_io": v((3, r, w), BF16),
        "w_self": v((3, w, w), BF16),
        "w_cross": v((3, w, w), BF16),
        "w_mix": v((2, w, w), BF16),
        "w_exp": v((z.ff, w), BF16),
        "w_shr": v((z.ff, w), BF16),
        "packed": v((3, z.slots, z.pcol), BF16),
        "landed": v((3, z.slots, z.pcol), BF16),
        "back": v((3, z.slots, z.pcol), BF16),
        "place": v((z.parts, z.slots, r), BF16),
        "place_t": v((z.parts, r, z.slots), BF16),
        "compact": v((z.lanes_packed, z.parts, r, z.slots), BF16),
        "row_local": v((r, 128), F32),
        "bias": v((2, k, r), F32),
        "all_rows": v((2, k, w), BF16),
        "query": v((2, r, w), BF16),
        "key": v((2, k, w), BF16),
        "value": v((2, k, w), BF16),
        "score": v((k, 2 * r), F32),
        "lifted": v((2, z.pairs, k, 2 * r), BF16),
        "mixed_t": v((2, z.pairs, PAIR, r), BF16),
        "inverse": v((2, z.pairs, 8, 2 * r), F32),
        "mixed": v((2, r, w), BF16),
        "unit": v((3, r, w), F32),
        "spread": v((3, r, 128), F32),
        "stream": v((r, w), F32),
        "stream_low": v((2, r, w), BF16),
        "grad_in": v((r, w), BF16),
        "grad_q": v((r, w), BF16),
        "held": v((2, 2 * r, w), BF16),
        "held_y": v((2, r, w), BF16),
        "arrived": v((z.land_rows, w), BF16),
        "norm_acc": v((z.stages + 1, 8, w), F32),
        "norm_in": v((z.stages, 8, w), F32),
        "arrival": v((z.n_dp * z.n_seq * r // 128, 128), jnp.int32),
        "lengths": pltpu.SMEM((z.n_dp * z.group_sents,), jnp.int32),
        "flags": pltpu.SMEM((z.n_dp * z.group_sents,), jnp.int32),
        "gains": v((3, w), F32),
        "shifts": v((3, w), F32),
        "load_sem": dma((8,)),
        "small_sem": dma((5,)),
        "in_send": dma((3,)),
        "in_recv": dma((3, 4)),
        "back_send": dma((3,)),
        "back_recv": dma((3, 4)),
        "all_send": dma((2, 3, 4)),
        "all_recv": dma((2, 3, 4)),
        "part_send": dma((2, 3)),
        "part_recv": dma((2, 3)),
        "sum_send": dma((n_units, z.stages)),
        "sum_recv": dma((n_units, z.stages)),
        "sum_free": pltpu.SemaphoreType.REGULAR((n_units, z.stages)),
        "full_send": dma(()),
        "full_recv": dma((n_units, z.stages)),
        "norm_send": dma((z.stages,)),
        "norm_recv": dma((z.stages,)),
    }


INPUTS = (
    "arrival_hbm",
    "lengths_hbm",
    "flags_hbm",
    "tokens",
    "memory",
    "cotangent",
    "self_proj",
    "cross_proj",
    "mixers",
    "expander",
    "shrinker",
    "gains_hbm",
    "shifts_hbm",
)
OUTPUTS = ("layer_out", "token_grad", "memory_grad", "sums", "g_norm")


class Refs:
    pass


def layer_kernel(z, names, *refs):
    t = Refs()
    for name, ref in zip(names, refs):
        setattr(t, name, ref)
    group = lax.axis_index("dp")
    lane = lax.axis_index("seq")
    device = group * z.n_seq + lane
    rows, width, keys = z.rows, z.width, z.keys
    wide = lambda value: jnp.concatenate([value, value], axis=1)
    def partner(axis, bit):
        index = group if axis == "dp" else lane
        step = 1 << bit
        high = lax.rem(lax.div(index, step), 2)
        other = index + step * (1 - 2 * high)
        return high, other, ((other, lane) if axis == "dp" else (group, other))

    inputs = [
        pltpu.make_async_copy(source, t.row_io.at[k], t.load_sem.at[k])
        for k, source in enumerate((t.tokens, t.memory, t.cotangent))
    ]
    weights = [
        pltpu.make_async_copy(t.self_proj, t.w_self, t.load_sem.at[3]),
        pltpu.make_async_copy(t.mixers, t.w_mix, t.load_sem.at[4]),
        pltpu.make_async_copy(t.cross_proj, t.w_cross, t.load_sem.at[5]),
        pltpu.make_async_copy(t.shrinker, t.w_shr, t.load_sem.at[6]),
    ]
    for j in range(z.ff_blocks):
        weights.append(
            pltpu.make_async_copy(
                t.expander.at[:, block(j, width)], t.w_exp.at[block(j, width)], t.load_sem.at[7]
            )
        )
    small = [
        pltpu.make_async_copy(getattr(t, name + "_hbm"), getattr(t, name), t.small_sem.at[i])
        for i, name in enumerate(("arrival", "lengths", "flags", "gains", "shifts"))
    ]
    for copy in small[:1] + inputs + small[1:]:
        copy.start()

    barrier = pltpu.get_barrier_semaphore()

    def greet(j, carry):
        to = lax.rem(group + j, z.n_dp)
        pl.semaphore_signal(barrier, inc=1, device_id=(to, lane), device_id_type=MESH)
        return carry

    lax.fori_loop(1, z.n_dp, greet, 0)
    for j in range(1, z.n_seq):
        to = lax.rem(lane + j, z.n_seq)
        pl.semaphore_signal(barrier, inc=1, device_id=(group, to), device_id_type=MESH)

    shift = (z.n_seq * rows).bit_length() - 1
    small[0].wait()
    strips = rows // 128
    mine = t.arrival[pl.ds(device * strips, strips), :]
    mine = jnp.concatenate([mine[i : i + 1] for i in range(strips)], axis=1)
    target = lax.shift_right_logical(mine, shift)
    hit = jnp.where(iota((z.n_dp, rows), 0) == target, 1.0, 0.0)
    earlier = jnp.where(iota((rows, rows), 0) < iota((rows, rows), 1), 1.0, 0.0).astype(BF16)
    rank = jnp.sum(hit * nn(hit.astype(BF16), earlier), axis=0, keepdims=True)
    place = target * z.prow + rank.astype(jnp.int32)
    for part in range(z.parts):
        picks = jnp.where(iota((z.slots, rows), 0) == place + part * z.cap, 1.0, 0.0)
        t.place[part] = picks.astype(BF16)

    def pack(k, selector, source):
        total = None
        for part in range(z.parts):
            piece = source[:, part * z.pcol : (part + 1) * z.pcol]
            term = nn(selector[part], piece)
            total = term if total is None else total + term
        t.packed[k] = total.astype(BF16)

    quarter_size = z.n_dp // 4
    quarter, member = lax.div(group, quarter_size), lax.rem(group, quarter_size)
    quarter_rows = quarter_size * z.prow

    def crossed(i):
        high = lax.rem(lax.div(quarter, 2) + i // 2, 2)
        return 2 * high + lax.rem(lax.rem(quarter, 2) + i % 2, 2)

    def send_rows(k, landing, send_sem, recv_sem):
        own = block(group, z.prow)
        done = recv_sem.at[k, quarter]
        pltpu.make_async_copy(t.packed.at[k, own], landing.at[k, own], done).start()
        for i in (3, 2, 1, 0):
            first = crossed(i) * quarter_size

            def one(j, carry):
                to = first + lax.rem(member + j, quarter_size)
                pltpu.make_async_remote_copy(
                    src_ref=t.packed.at[k, block(to, z.prow)],
                    dst_ref=landing.at[k, own],
                    send_sem=send_sem.at[k],
                    recv_sem=done,
                    device_id=(to, lane),
                    device_id_type=MESH,
                ).start()
                return carry

            lax.fori_loop(1 if i == 0 else 0, quarter_size, one, 0)

    def wait_quarter(k, landing, recv_sem, i):
        which = crossed(i)
        at = landing.at[k, block(which, quarter_rows)]
        pltpu.make_async_copy(at, at, recv_sem.at[k, which]).wait()
        return block(which, quarter_rows)

    def wait_rows(k, landing, recv_sem):
        for i in range(4):
            wait_quarter(k, landing, recv_sem, i)

    def wait_sent(k, send_sem):
        others = pl.ds(0, (z.n_dp - 1) * z.prow)
        pltpu.make_async_copy(
            t.packed.at[k, others], t.packed.at[k, others], send_sem.at[k]
        ).wait()

    inputs[0].wait()
    pack(0, t.place, t.row_io[0])
    pl.semaphore_wait(barrier, z.n_dp - 1 + z.n_seq - 1)

    running, gathered, landed_count, exchanged, given = {}, {}, {}, set(), []

    def advance(name):
        try:
            next(running[name])
        except StopIteration:
            del running[name]

    def begin(name, task):
        next(task)
        running[name] = task

    def step(piece):
        if not z.planned:
            for name in list(running):
                advance(name)
            return
        for name in PLAN.get(piece, ()):
            if name in (X1, X2):
                start_exchange(1 + name - X1)
            elif name in running:
                advance(name)

    def finish(done=lambda: False):
        while running and not done():
            for name in list(running):
                advance(name)

    def start_exchange(k):
        if k in exchanged:
            return
        exchanged.add(k)
        send_rows(k, t.landed, t.in_send, t.in_recv)
        if z.passes and k < 2:
            for i in range(4):
                begin(P00 + 4 * k + i, pass_on(k, i))

    near_lane, near = partner("seq", 0)[1:]
    far_lane, far = partner("seq", 1)[1:]
    lanes = (lane, near_lane, far_lane, near_lane + (far_lane - lane))

    def passing(k, source, at, which, sem, to):
        return pltpu.make_async_remote_copy(
            src_ref=source.at[at],
            dst_ref=t.passed.at[k, which, at],
            send_sem=t.all_send.at[k, which, sem],
            recv_sem=t.all_recv.at[k, which, sem],
            device_id=to,
            device_id_type=MESH,
        )

    def pass_on(k, i):
        yield
        at = wait_quarter(k, t.landed, t.in_recv, i)
        landed_count[k] = landed_count.get(k, 0) + 1
        to_far = passing(k, t.landed.at[k], at, 0, i, far)
        to_far.start()
        yield
        to_far.wait()
        gathered[k, 0] = gathered.get((k, 0), 0) + 1
        if i % 2 == 1:
            half_at = block(lax.div(crossed(i), 2), 2 * quarter_rows)
            relay = passing(k, t.passed.at[k, 0], half_at, 2, i // 2, near)
            relay.start()
            yield
            relay.wait()
            gathered[k, 2] = gathered.get((k, 2), 0) + 2

    def pass_near(k):
        to_near = passing(k, t.landed.at[k], pl.ds(0, z.slots), 1, 0, near)
        to_near.start()
        yield
        to_near.wait()
        gathered[k, 1] = 4

    start_exchange(0)
    for copy in weights:
        copy.start()
    step(START)
    for k in (1, 2):
        inputs[k].wait()
        pack(k, t.place, t.row_io[k])
        step(PACK1 + k - 1)

    place_down = jnp.transpose(jnp.broadcast_to(place.astype(F32), (128, rows)))[:, 0:1].astype(jnp.int32)
    for part in range(z.parts):
        picks = jnp.where(iota((rows, z.slots), 1) == place_down + part * z.cap, 1.0, 0.0)
        t.place_t[part] = picks.astype(BF16)
    step(PLACE)
    n_all = z.n_dp * z.n_seq
    arrival = [t.arrival[pl.ds(i, n_all, stride=strips), :] for i in range(strips)]
    arrival = jnp.concatenate(arrival, axis=1)
    whose = lax.shift_right_logical(arrival, shift)
    ours = jnp.where(whose == group, 1.0, 0.0)
    local = (arrival - whose * (z.n_seq * rows)).astype(F32)
    within = nn(ours.astype(BF16), earlier)
    key_local = t.score.at[:, 0:128]
    rank_at = t.bias.at[0, 0:n_all, :]
    local_at = t.bias.at[0, n_all : 2 * n_all, :]
    rank_at[...] = jnp.where(ours > 0.5, within, -1.0)
    local_at[...] = local
    digits = t.lifted.at[1, 0]

    def slot_locals(index):
        chosen = rank_at[pl.ds(index, 1), :] == iota((z.prow, rows), 0).astype(F32)
        found = jnp.where(chosen, local_at[pl.ds(index, 1), :], 0.0)
        found = jnp.sum(found, axis=1, keepdims=True)
        high = jnp.floor(found * (1.0 / 32))
        pair = jnp.where(iota((z.prow, 128), 1) == 0, high, found - 32.0 * high)
        source, other = index // z.n_seq, index % z.n_seq
        digits[block(source, z.prow), block(other, 128)] = pair.astype(BF16)

    loop(n_all, slot_locals)
    step(SLOTS)
    down, across = iota((n_all, n_all), 0), iota((n_all, n_all), 1)
    same_lane = (down & (z.n_seq - 1)) == (across & (z.n_seq - 1))
    count_row = nt(jnp.ones((16, rows), BF16), ours.astype(BF16))
    after = jnp.where(same_lane & (down < across), 1.0, 0.0).astype(BF16)
    base_row = nn(count_row.astype(BF16), after)
    first_row = jnp.where(count_row > 0.5, base_row, -1024.0).astype(BF16)
    in_block = iota((1, z.slots), 1) & (z.prow - 1)
    from_source = lax.shift_right_logical(iota((n_all, z.slots), 1), z.prow.bit_length() - 1)
    for index in range(z.n_seq):
        wanted = from_source * z.n_seq + lanes[index]
        expand = jnp.where(iota((n_all, z.slots), 0) == wanted, 1.0, 0.0).astype(BF16)
        spot_row = nn(first_row, expand)[0:1, :].astype(jnp.int32)
        for part in range(z.parts):
            offset = in_block - part * z.cap
            spot = jnp.where((offset >= 0) & (offset < z.cap), spot_row + offset, -1)
            picks = jnp.where(spot == iota((rows, z.slots), 0), 1.0, 0.0).astype(BF16)
            if index < z.lanes_packed:
                t.compact[index, part] = picks
            if part == 0:
                found = nn(picks, digits[0 : z.slots, block(lanes[index], 128)])
                found = 32.0 * found[:, 0:1] + found[:, 1:2]
                key_local[block(lanes[index], rows), :] = jnp.broadcast_to(found, (rows, 128))
            if index == 0:
                spot_tall = jnp.broadcast_to(spot.astype(F32), (128, z.slots))
                spot_down = jnp.transpose(spot_tall)[:, 0:1].astype(jnp.int32)
                picks = jnp.where(spot_down == iota((z.slots, rows), 1), 1.0, 0.0)
                t.place[part] = picks.astype(BF16)
        step(LANE0 + index)

    def sentence_of(index):
        start, end, weight = jnp.zeros_like(index), jnp.zeros_like(index), jnp.zeros_like(index)
        edge = 0
        for j in range(z.group_sents):
            sentence = group * z.group_sents + j
            after = edge + t.lengths[sentence]
            low, high = jnp.float32(edge), after.astype(F32)
            share = jnp.where(t.flags[sentence] == 1, 1.0, SYNTH_WEIGHT)
            here = index >= low
            start = jnp.where(here, low, start)
            end = jnp.where(here, high, end)
            weight = jnp.where(here, share, weight)
            edge = after
        return start, end, weight

    for copy in small[1:]:
        copy.wait()
    own_local = key_local[block(lane, rows), :]
    t.row_local[...] = sentence_of(own_local)[2]
    query_local = jnp.transpose(own_local)[0:1, :]
    query_start, query_end, _ = sentence_of(query_local)

    def make_bias(j):
        here = key_local[block(j, rows), 0:1]
        late = here >= query_start
        t.bias[0, block(j, rows), :] = jnp.where(late & (here <= query_local), 0.0, SCORE_FILL)
        t.bias[1, block(j, rows), :] = jnp.where(late & (here < query_end), 0.0, SCORE_FILL)

    loop(z.n_seq, make_bias)
    step(BIAS)

    def unpack(selector, source):
        pieces = [nn(selector[part], source) for part in range(z.parts)]
        return pieces[0] if z.parts == 1 else jnp.concatenate(pieces, axis=1)

    def gather_seq(k):
        held = t.all_rows

        def copy(what, which, to):
            return pltpu.make_async_remote_copy(
                src_ref=held.at[k, what],
                dst_ref=held.at[k, what],
                send_sem=t.all_send.at[k, which, 0],
                recv_sem=t.all_recv.at[k, which, 0],
                device_id=to,
                device_id_type=MESH,
            )

        ours = block(lane, rows)
        to_far, to_near = copy(ours, 0, far), copy(ours, 1, near)
        relay = copy(block(far_lane, rows), 2, near)
        to_far.start()
        to_near.start()
        yield
        to_near.wait()
        to_far.wait()
        relay.start()
        gathered[k, 0] = gathered[k, 1] = 4
        yield
        relay.wait()
        gathered[k, 2] = 4

    def own_rows(k):
        if z.passes:
            finish(lambda: landed_count.get(k) == 4)
            begin(N0 + k, pass_near(k))
        else:
            wait_rows(k, t.landed, t.in_recv)
        t.all_rows[k, block(lane, rows), :] = unpack(t.compact.at[0], t.landed[k]).astype(BF16)
        if not z.passes:
            begin(N0 + k, gather_seq(k))

    def other_rows(k, which):
        finish(lambda: gathered.get((k, which)) == 4)
        index = (2, 1, 3)[which]
        if z.passes:
            found = unpack(t.compact.at[index], t.passed[k, which]).astype(BF16)
            t.all_rows[k, block(lanes[index], rows), :] = found
        return lanes[index]

    lanes_low = iota((rows, PAIR), 1) < HEAD
    tall_low = iota((PAIR, rows), 0) < HEAD
    none = jnp.zeros((), BF16)

    def stacked_queries(branch, p):
        pair = t.query[branch, :, block(p, PAIR)]
        return jnp.concatenate(
            [jnp.where(lanes_low, pair, none), jnp.where(lanes_low, none, pair)], axis=0
        )

    def stacked_tall(tall):
        return jnp.concatenate(
            [jnp.where(tall_low, tall, 0.0), jnp.where(tall_low, 0.0, tall)], axis=1
        )

    def split_pair(both):
        return jnp.concatenate([both[:HEAD, :rows], both[HEAD:, rows:]], axis=0)

    def attend_pair(branch, p):
        cols = block(p, PAIR)
        tall = jnp.transpose(t.query[branch, :, cols].astype(F32))
        stacked = stacked_tall(tall).astype(BF16)

        def scores(j, peak):
            at = block(j, rows)
            score = nn(t.key[branch, at, cols], stacked) + wide(t.bias[branch, at, :])
            t.score[at, :] = score
            return jnp.maximum(peak, jnp.max(score, axis=0, keepdims=True))

        peak = jnp.full((1, 2 * rows), -3e38, F32)
        for j in range(z.n_seq):
            peak = scores(j, peak)

        def lift(j, carry):
            total, mixed = carry
            at = block(j, rows)
            lifted = jnp.exp(t.score[at, :] - peak)
            low = lifted.astype(BF16)
            t.lifted[branch, p, at, :] = low
            return (
                total + jnp.sum(lifted, axis=0, keepdims=True),
                mixed + tn(t.value[branch, at, cols], low),
            )

        sums = (jnp.zeros((1, 2 * rows), F32), jnp.zeros((PAIR, 2 * rows), F32))
        for j in range(z.n_seq):
            sums = lift(j, sums)
        total, mixed = sums
        inverse = 1.0 / total
        t.inverse[branch, p] = jnp.broadcast_to(inverse, (8, 2 * rows))
        tall = split_pair(mixed * inverse)
        t.mixed_t[branch, p] = tall.astype(BF16)
        t.mixed[branch, :, cols] = jnp.transpose(tall).astype(BF16)

    def attend_back_pair(branch, p):
        cols = block(p, PAIR)
        stacked = stacked_queries(branch, p)
        inverse = t.inverse[branch, p, 0:1, :]
        tall = jnp.transpose(t.grad_in[:, cols].astype(F32))
        product = tall * t.mixed_t[branch, p].astype(F32)
        inner = inverse * jnp.concatenate(
            [
                jnp.sum(product[:HEAD], axis=0, keepdims=True),
                jnp.sum(product[HEAD:], axis=0, keepdims=True),
            ],
            axis=1,
        )
        both = stacked_tall(tall) * inverse
        both_down = jnp.transpose(both).astype(BF16)
        both = both.astype(BF16)

        def one(j, query_grad):
            at = block(j, rows)
            low = t.lifted[branch, p, at, :]
            prob_grad = nn(t.value[branch, at, cols], both)
            score_grad = (low.astype(F32) * (prob_grad - inner)).astype(BF16)
            t.w_shr[at, cols] = nn(score_grad, stacked).astype(BF16)
            t.w_shr[rows_at(keys + j * rows, rows), cols] = nn(low, both_down).astype(BF16)
            return query_grad + tn(t.key[branch, at, cols], score_grad)

        query_grad = jnp.zeros((PAIR, 2 * rows), F32)
        for j in range(z.n_seq):
            query_grad = one(j, query_grad)
        tall_grad = split_pair(query_grad) * HEAD ** (-0.5)
        t.grad_q[:, cols] = jnp.transpose(tall_grad).astype(BF16)

    def project_keys(branch, weight, j):
        at = block(j, rows)
        source = t.all_rows[branch, at, :]
        t.key[branch, at, :] = nn(source, weight[1]).astype(BF16)
        t.value[branch, at, :] = nn(source, weight[2]).astype(BF16)

    def norm_forward(values, i):
        center = values - jnp.sum(values, axis=-1, keepdims=True) * (1.0 / width)
        var = jnp.sum(center * center, axis=-1, keepdims=True) * (1.0 / width)
        scale = lax.rsqrt(var + EPSILON)
        unit = center * scale
        t.unit[i] = unit
        t.spread[i] = jnp.broadcast_to(scale, (rows, 128))
        return unit * t.gains[i : i + 1, :] + t.shifts[i : i + 1, :]

    def norm_backward(grad, i):
        unit = t.unit[i]
        t.norm_acc[0, i : i + 1, :] = jnp.sum(grad * unit, axis=0, keepdims=True)
        t.norm_acc[0, 3 + i : 4 + i, :] = jnp.sum(grad, axis=0, keepdims=True)
        scaled = grad * t.gains[i : i + 1, :]
        mean = jnp.sum(scaled, axis=-1, keepdims=True) * (1.0 / width)
        slope = jnp.sum(scaled * unit, axis=-1, keepdims=True) * (1.0 / width)
        return (scaled - mean - unit * slope) * t.spread[i, :, 0:1]

    def add_rows(offset, spot, count, cols):
        tile = next(s for s in (128, 96, 64, 48, 32, 16) if count % s == 0)

        def one(i):
            at = rows_at(offset + i * tile, tile)
            t.sums[at, cols] += t.arrived[rows_at(spot + i * tile, tile), cols]

        loop(count // tile, one)

    def sum_unit(name):
        unit, offset, count, first_col, n_cols, order = z.units[name]
        cols = pl.ds(first_col, n_cols)
        spot = z.land[name]
        halved = []
        for s, (axis, bit) in enumerate(order):
            high, _, to = partner(axis, bit)
            halving = z.halves(count, s)
            if halving:
                count //= 2
                keep, give = offset + high * count, offset + (1 - high) * count
                halved.append((s, high, to, axis, bit))
            else:
                keep = give = offset
            copy = pltpu.make_async_remote_copy(
                src_ref=t.sums.at[rows_at(give, count), cols],
                dst_ref=t.arrived.at[rows_at(spot, count), cols],
                send_sem=t.sum_send.at[unit, s],
                recv_sem=t.sum_recv.at[unit, s],
                device_id=to,
                device_id_type=MESH,
            )
            copy.start()
            yield
            copy.wait()
            if halving:
                pl.semaphore_signal(
                    t.sum_free.at[unit, s], inc=1, device_id=to, device_id_type=MESH
                )
            add_rows(keep, spot, count, cols)
            offset = keep
            spot += count
        for s, high, to, axis, bit in reversed(halved):
            held = t.sums.at[rows_at(offset, count), cols]
            copy = pltpu.make_async_remote_copy(
                src_ref=held,
                dst_ref=held,
                send_sem=t.full_send,
                recv_sem=t.full_recv.at[unit, s],
                device_id=to,
                device_id_type=MESH,
            )
            pl.semaphore_wait(t.sum_free.at[unit, s], 1)
            copy.start()
            given.append(count)
            yield
            copy.wait_recv()
            offset = offset - high * count
            count *= 2

    def sum_norms():
        for s, (axis, bit) in enumerate(z.order_a):
            _, _, to = partner(axis, bit)
            copy = pltpu.make_async_remote_copy(
                src_ref=t.norm_acc.at[s],
                dst_ref=t.norm_in.at[s],
                send_sem=t.norm_send.at[s],
                recv_sem=t.norm_recv.at[s],
                device_id=to,
                device_id_type=MESH,
            )
            copy.start()
            yield
            copy.wait()
            t.norm_acc[s + 1] = t.norm_acc[s] + t.norm_in[s]
        t.g_norm[...] = t.norm_acc[z.stages]

    def return_rows(k):
        wait_sent(k, t.in_send)
        pack(k, t.place, t.row_io[k])
        send_rows(k, t.back, t.back_send, t.back_recv)

    def return_part(branch, k, result):
        first = branch * keys
        cross_lane = lanes[3]

        def at(which):
            return rows_at(first + which * rows, rows)

        def copy(source, landing, which, to):
            return pltpu.make_async_remote_copy(
                src_ref=source,
                dst_ref=landing,
                send_sem=t.part_send.at[branch, which],
                recv_sem=t.part_recv.at[branch, which],
                device_id=to,
                device_id_type=MESH,
            )

        one = copy(t.w_exp.at[at(cross_lane)], t.held.at[branch, pl.ds(rows, rows)], 0, near)
        two = copy(t.w_exp.at[at(near_lane)], t.held.at[branch, pl.ds(0, rows)], 1, near)
        one.start()
        two.start()
        yield
        one.wait()
        t.w_exp[at(far_lane), :] = (
            t.w_exp[at(far_lane), :].astype(F32) + t.held[branch, rows:, :].astype(F32)
        ).astype(BF16)
        three = copy(t.w_exp.at[at(far_lane)], t.held_y.at[branch], 2, far)
        three.start()
        two.wait()
        yield
        three.wait()
        total = (
            t.w_exp[at(lane), :].astype(F32)
            + t.held[branch, :rows, :].astype(F32)
            + t.held_y[branch].astype(F32)
        )
        t.row_io[k] = total.astype(BF16)
        yield from bring_back(k, result)

    def bring_back(k, result):
        return_rows(k)
        yield
        wait_rows(k, t.back, t.back_recv)
        wait_sent(k, t.back_send)
        result[...] = unpack(t.place_t, t.back[k]).astype(BF16)

    def put_sum(name, j, value):
        first = z.units[name][1] + j * width
        t.sums[pl.ds(first, width), :] = value.astype(BF16)

    own = block(lane, rows)
    own_rows(0)
    start_exchange(1)
    step(OWN0)
    weights[0].wait()
    tokens = t.all_rows[0, own, :]
    t.query[0] = (nn(tokens, t.w_self[0]).astype(BF16).astype(F32) * HEAD ** (-0.5)).astype(BF16)
    project_keys(0, t.w_self, lane)
    step(Q0)
    for which, piece in ((1, NEAR0), (0, FAR0), (2, DIAG0)):
        project_keys(0, t.w_self, other_rows(0, which))
        step(piece)
    half = z.pairs // 2
    loop(half, functools.partial(attend_pair, 0))
    step(SATT0)
    loop(z.pairs - half, lambda p: attend_pair(0, half + p))
    step(SATT1)
    weights[1].wait()
    weights[2].wait()
    first = norm_forward(t.all_rows[0, own, :].astype(F32) + nn(t.mixed[0], t.w_mix[0]), 0)
    t.stream[...] = first
    t.stream_low[0] = first.astype(BF16)
    step(LN0)
    cross_query = nn(t.stream_low[0], t.w_cross[0]).astype(BF16)
    t.query[1] = (cross_query.astype(F32) * HEAD ** (-0.5)).astype(BF16)
    step(CQ)
    own_rows(1)
    start_exchange(2)
    step(OWN1)
    project_keys(1, t.w_cross, lane)
    step(KV1)
    for which, piece in ((1, NEAR1), (0, FAR1), (2, DIAG1)):
        project_keys(1, t.w_cross, other_rows(1, which))
        step(piece)
    loop(half, functools.partial(attend_pair, 1))
    step(CATT0)
    loop(z.pairs - half, lambda p: attend_pair(1, half + p))
    step(CATT1)

    second = norm_forward(t.stream[...] + nn(t.mixed[1], t.w_mix[1]), 1)
    t.stream[...] = second
    t.stream_low[1] = second.astype(BF16)
    for copy in weights[3:]:
        copy.wait()
    step(LN1)

    def hidden_at(j):
        if z.passes:
            return t.passed.at[0, j // 2, block(j % 2, rows), :]
        return t.hidden.at[j]

    def expand_block(j):
        pre = nn(t.stream_low[1], t.w_exp[block(j, width), :])
        gate = 0.5 + 0.5 * jnp.tanh(0.5 * pre)
        hidden = (pre * gate).astype(BF16)
        hidden_at(j)[...] = hidden
        t.score[block(j, rows), :] = gate * (1.0 + pre * (1.0 - gate))
        t.stream[...] += nn(hidden, t.w_shr[block(j, width), :])

    half = z.ff_blocks // 2
    for part in range(2):
        for j in range(half):
            expand_block(part * half + j)
        step(FFN0 + part)
    t.row_io[0] = norm_forward(t.stream[...], 2).astype(BF16)
    begin(OUT, bring_back(0, t.layer_out))
    step(LN2)

    wait_rows(2, t.landed, t.in_recv)
    grad = unpack(t.compact.at[0], t.landed[2]) * t.row_local[:, 0:1]
    t.stream[...] = norm_backward(grad, 2)
    t.grad_in[...] = t.stream[...].astype(BF16)
    step(COT)

    half = z.ff_blocks // 2
    for part, name in enumerate((SHR0, SHR1)):
        for j in range(half):
            put_sum(name, j, tn(hidden_at(part * half + j)[...], t.grad_in[...]))
        begin(name, sum_unit(name))
        step(FB0 + part)

    def expand_back(part, j, name):
        cols = block(part * half + j, width)
        pre_grad = nt(t.grad_in[...], t.w_shr[cols, :]) * t.score[block(part * half + j, rows), :]
        low = pre_grad.astype(BF16)
        put_sum(name, j, tn(t.stream_low[1], low))
        t.stream[...] += nt(low, t.w_exp[cols, :])

    for part, name in enumerate((EXP0, EXP1)):
        for j in range(half):
            expand_back(part, j, name)
        begin(name, sum_unit(name))
        step(FB2 + part)
    t.stream[...] = norm_backward(t.stream[...], 1)
    low = t.stream[...].astype(BF16)
    put_sum(CROSS_Q, 0, tn(t.mixed[1], low))
    t.grad_in[...] = nt(low, t.w_mix[1]).astype(BF16)
    step(LN1B)

    def row_part(branch, weight):
        def one(j):
            at = block(j, rows)
            total = nt(t.w_shr[at, :], weight[1]) + nt(
                t.w_shr[rows_at(keys + j * rows, rows), :], weight[2]
            )
            t.w_exp[rows_at(branch * keys + j * rows, rows), :] = total.astype(BF16)

        loop(z.n_seq, one)

    def key_sums(branch, which):
        first = which * keys

        def one(j, total):
            return total + tn(
                t.all_rows[branch, block(j, rows), :], t.w_shr[rows_at(first + j * rows, rows), :]
            )

        return lax.fori_loop(0, z.n_seq, one, jnp.zeros((width, width), F32))

    def attention_back(branch, weight, first, source, k, result):
        q_sum, kv_sum = ((SELF_Q, SELF_KV), (CROSS_Q, CROSS_KV))[branch]
        half = z.pairs // 2
        for part in range(2):
            loop(half, lambda p: attend_back_pair(branch, part * half + p))
            step(first + part)
        row_part(branch, weight)
        if branch == 0:
            t.w_exp[own, :] = (
                t.w_exp[own, :].astype(F32) + t.stream[...] + nt(t.grad_q[...], weight[0])
            ).astype(BF16)
        begin(RET0 + branch, return_part(branch, k, result))
        step(first + 2)
        put_sum(q_sum, 1, tn(source[...], t.grad_q[...]))
        begin(q_sum, sum_unit(q_sum))
        step(first + 3)
        put_sum(kv_sum, 0, key_sums(branch, 0))
        step(first + 4)
        put_sum(kv_sum, 1, key_sums(branch, 1))
        begin(kv_sum, sum_unit(kv_sum))
        step(first + 5)

    attention_back(1, t.w_cross, CROSS_B0, t.stream_low.at[0], 2, t.memory_grad)
    t.stream[...] = norm_backward(t.stream[...] + nt(t.grad_q[...], t.w_cross[0]), 0)
    t.norm_acc[0, 6:8, :] = jnp.zeros((2, width), F32)
    begin(NORM, sum_norms())
    step(LN0B)
    low = t.stream[...].astype(BF16)
    put_sum(SELF_Q, 0, tn(t.mixed[0], low))
    t.grad_in[...] = nt(low, t.w_mix[0]).astype(BF16)
    step(MIX0)
    attention_back(0, t.w_self, SELF_B0, t.all_rows.at[0, own], 1, t.token_grad)
    finish()
    total = t.sums.at[pl.ds(0, sum(given)), :]
    pltpu.make_async_copy(total, total, t.full_send).wait()


def finish_kernel(z, *refs):
    w = z.width
    sums, rows, norms = refs[0], refs[1:4], refs[4]
    g_self, g_cross, g_mix, g_exp, g_shr = refs[5:10]
    done, gains, shifts, full, out_sem, row_sem = refs[10:13], *refs[13:]
    copies = [pltpu.make_async_copy(a, b, row_sem.at[i]) for i, (a, b) in enumerate(zip(rows, done))]
    for copy in copies:
        copy.start()
    gains[...] = norms[0:3, :]
    shifts[...] = norms[3:6, :]
    pieces = []
    half = z.ff_blocks // 2
    for j in range(z.ff_blocks):
        for name, result in (((SHR0, SHR1)[j // half], g_shr), ((EXP0, EXP1)[j // half], g_exp)):
            spot = (block(j, w), slice(None)) if result is g_shr else (slice(None), block(j, w))
            pieces.append((z.units[name][1] + (j % half) * w, result.at[spot]))
    for j, (name, result) in enumerate(((SELF_Q, g_self), (CROSS_Q, g_cross))):
        first = z.units[name][1]
        pieces.append((first, g_mix.at[j]))
        pieces += [(first + (1 + i) * w, result.at[i]) for i in range(3)]

    def widen(first, i):
        def one(c):
            at = rows_at(first + c * 64, 64)
            full[i, block(c, 64), :] = sums[at, :].astype(F32)

        loop(w // 64, one)

    for i, (first, result) in enumerate(pieces):
        widen(first, i)
        copy = pltpu.make_async_copy(full.at[i], result, out_sem.at[i])
        copy.start()
        copies.append(copy)
    for copy in copies:
        copy.wait()


def body(
    z,
    tokens,
    memory,
    cotangent,
    arrival_order,
    lengths,
    real_flag,
    self_proj,
    cross_proj,
    mixers,
    expander,
    shrinker,
    norm_gains,
    norm_shifts,
):
    scratch = scratch_list(z)
    names = INPUTS + OUTPUTS + tuple(scratch)
    w = z.width
    anywhere = pl.BlockSpec(memory_space=pl.ANY)
    vmem = pl.BlockSpec(memory_space=pltpu.VMEM)
    results = pl.pallas_call(
        functools.partial(layer_kernel, z, names),
        out_shape=(pltpu.VMEM((z.rows, w), BF16),) * 3
        + (pltpu.VMEM((z.sum_rows, w), BF16), pltpu.VMEM((8, w), F32)),
        in_specs=[anywhere] * 13,
        out_specs=[vmem] * 5,
        scratch_shapes=list(scratch.values()),
        compiler_params=pltpu.CompilerParams(
            collective_id=0, has_side_effects=True, vmem_limit_bytes=LAYER_VMEM
        ),
        name="layer",
    )(
        arrival_order.reshape(-1, 128),
        lengths,
        real_flag,
        tokens,
        memory,
        cotangent,
        self_proj,
        cross_proj,
        mixers,
        expander,
        shrinker,
        norm_gains,
        norm_shifts,
    )
    *row_results, sums, norms = results
    n_blocks = z.sum_rows // w
    wide = [(3, w, w), (3, w, w), (2, w, w), (w, z.ff), (z.ff, w)]
    done = pl.pallas_call(
        functools.partial(finish_kernel, z),
        out_shape=tuple(jax.ShapeDtypeStruct(shape, F32) for shape in wide)
        + (jax.ShapeDtypeStruct((z.rows, w), BF16),) * 3
        + (jax.ShapeDtypeStruct((3, w), F32),) * 2,
        in_specs=[vmem] * 5,
        out_specs=[anywhere] * 8 + [vmem] * 2,
        scratch_shapes=[
            pltpu.VMEM((n_blocks, w, w), F32),
            pltpu.SemaphoreType.DMA((n_blocks,)),
            pltpu.SemaphoreType.DMA((3,)),
        ],
        compiler_params=pltpu.CompilerParams(vmem_limit_bytes=FINISH_VMEM),
        name="widen",
    )(sums, *row_results, norms)
    return (*done[5:8], *done[:5], *done[8:])


def solution(mesh):
    n_dp, n_seq = mesh.shape["dp"], mesh.shape["seq"]

    def whole(*arrays):
        tokens, lengths, expander = arrays[0], arrays[4], arrays[9]
        z = Sizes(
            n_dp,
            n_seq,
            tokens.shape[0] // (n_dp * n_seq),
            tokens.shape[1],
            expander.shape[1],
            lengths.shape[0],
        )
        split = P(("dp", "seq"), None)
        return jax.shard_map(
            functools.partial(body, z),
            mesh=mesh,
            in_specs=(split,) * 3 + (P(),) * 10,
            out_specs=(split,) * 3 + (P(),) * 7,
            check_vma=False,
        )(*arrays)

    return whole
```

```python
import functools

import jax
import jax.numpy as jnp
from jax import lax
from jax.experimental import pallas as pl
from jax.experimental.pallas import tpu as pltpu
from jax.sharding import PartitionSpec as P

HEAD = 64
PAIR = 2 * HEAD
MESH = pl.DeviceIdType.MESH
F32 = jnp.float32
BF16 = jnp.bfloat16
EPSILON = 1e-05
SYNTH_WEIGHT = 0.4
SCORE_FILL = -1e30
LAYER_VMEM = 55 * 1024 * 1024
FINISH_VMEM = 24 * 1024 * 1024

(
    P00, P01, P02, P03, P10, P11, P12, P13, N0, N1, X1, X2,
    OUT, RET0, RET1, NORM, SHR0, EXP0, SHR1, EXP1, CROSS_Q, CROSS_KV,
    SELF_Q, SELF_KV,
) = range(24)
(
    START, PACK1, PACK2, PLACE, SLOTS, LANE0, LANE1, LANE2, LANE3, BIAS,
    OWN0, Q0, NEAR0, FAR0, DIAG0, SATT0, SATT1, LN0, CQ, OWN1,
    KV1, NEAR1, FAR1, DIAG1, CATT0, CATT1, LN1, FFN0, FFN1, LN2,
    COT, FB0, FB1, FB2, FB3, LN1B, CROSS_B0, CROSS_B1, CROSS_ROW, CROSS_SQ,
    CROSS_SK, CROSS_SV, LN0B, MIX0, SELF_B0, SELF_B1, SELF_ROW, SELF_SQ, SELF_SK, SELF_SV,
) = range(50)
PLAN = {
    LANE0: (P00,),
    LANE1: (P01,),
    BIAS: (P02, X1, P00, P03),
    Q0: (P01, P02, N0, P10, P01),
    NEAR0: (P03,),
    FAR0: (P11, P12, P03),
    SATT1: (P13,),
    OWN1: (X2, P10),
    KV1: (P12, P11, P13, N1),
    FAR1: (P11, P13),
    LN1B: (SHR0,),
    CROSS_B1: (EXP1,),
    CROSS_SQ: (SHR1, EXP0),
    LN0B: (EXP1,),
    MIX0: (RET1, CROSS_Q, CROSS_KV, SHR0),
    SELF_B1: (RET1,),
    SELF_ROW: (EXP0,),
    SELF_SQ: (CROSS_KV, CROSS_Q),
    SELF_SK: (SHR0,),
    SELF_SV: (
        SELF_Q, EXP0, SHR0, CROSS_Q, SELF_KV, EXP1, EXP0, RET0,
        SHR0, SELF_Q, CROSS_KV, CROSS_Q, SHR0, SELF_KV, EXP0, EXP1,
        SELF_Q, SHR1, CROSS_Q, EXP0, CROSS_KV, EXP1, SELF_KV, SHR0,
        SELF_Q, CROSS_Q, SHR1, NORM, SELF_KV, CROSS_KV, EXP1, SELF_Q,
        EXP0, SHR1, CROSS_Q, SELF_Q, SHR0, RET1, SELF_KV, EXP1,
        CROSS_KV, SHR1, EXP0, NORM, SELF_KV, CROSS_KV, SELF_Q, SHR1,
        CROSS_Q, SELF_KV, RET0, EXP1, CROSS_Q, SHR1, EXP0, CROSS_KV,
        SELF_Q, EXP1, SHR0, NORM, OUT, SELF_KV, SELF_Q, SHR1,
        NORM, CROSS_KV, SELF_KV, RET0, NORM, SHR1,
    ),
}
ORDERS = {
    SHR0: (0, 2, 1, 3, 4),
    EXP0: (0, 1, 2, 3, 4),
    SHR1: (0, 2, 1, 3, 4),
    EXP1: (0, 1, 3, 2, 4),
    CROSS_Q: (0, 2, 1, 3, 4),
    CROSS_KV: (0, 3, 2, 1, 4),
    SELF_Q: (0, 2, 3, 1, 4),
    SELF_KV: (0, 1, 2, 3, 4),
}


def contract(a, b, left, right):
    return lax.dot_general(a, b, (((left,), (right,)), ((), ())), preferred_element_type=F32)


def nn(a, b):
    return contract(a, b, 1, 0)


def nt(a, b):
    return contract(a, b, 1, 1)


def tn(a, b):
    return contract(a, b, 0, 0)


def block(index, size):
    if isinstance(index, int):
        return pl.ds(index * size, size)
    return pl.ds(pl.multiple_of(index * size, size), size)


def rows_at(offset, size):
    if isinstance(offset, int):
        return pl.ds(offset, size)
    return pl.ds(pl.multiple_of(offset, 16), size)


def loop(count, step):
    def body(index, carry):
        step(index)
        return carry

    lax.fori_loop(0, count, body, 0)


def iota(shape, axis):
    return lax.broadcasted_iota(jnp.int32, shape, axis)


class Sizes:
    def __init__(self, n_dp, n_seq, rows, width, ff, sentences):
        self.n_dp, self.n_seq, self.rows, self.width, self.ff = n_dp, n_seq, rows, width, ff
        self.cap = 2 * rows // n_dp
        self.group_sents = sentences // n_dp
        self.parts = max(1, 16 // self.cap)
        self.prow = self.cap * self.parts
        self.pcol = width // self.parts
        self.slots = n_dp * self.prow
        self.passes = self.parts == 1
        self.lanes_packed = n_seq if self.passes else 1
        self.keys = n_seq * rows
        self.pairs = width // PAIR
        self.ff_blocks = ff // width
        lane_bits = [("seq", b) for b in range(n_seq.bit_length() - 1)]
        dp_bits = [("dp", b) for b in range(n_dp.bit_length() - 1)]
        self.planned = (n_dp, n_seq) == (8, 4)
        links = (("seq", 0), ("dp", 0), ("seq", 1), ("dp", 1), ("dp", 2))
        self.order_a = lane_bits[:1] + dp_bits[:2] + lane_bits[1:] + dp_bits[2:]
        self.order_b = lane_bits + dp_bits[1:2] + dp_bits[:1] + dp_bits[2:]
        self.stages = len(self.order_a)
        w = width
        self.units, row = {}, 0
        half = self.ff_blocks // 2
        names = [(name, half) for name in (SHR0, EXP0, SHR1, EXP1)]
        names += [(name, 2) for name in (CROSS_Q, CROSS_KV, SELF_Q, SELF_KV)]
        for name, blocks in names:
            order = (self.order_a, self.order_b)[len(self.units) % 2]
            if self.planned:
                order = [links[c] for c in ORDERS[name]]
            self.units[name] = (len(self.units), row, blocks * w, 0, w, order)
            row += blocks * w
        self.sum_rows = row
        self.land, spot = {}, 0
        for name, (_, _, count, _, _, _) in self.units.items():
            self.land[name] = spot
            n = count
            for s in range(self.stages):
                n = n // 2 if self.halves(n, s) else n
                spot += n
        self.land_rows = spot

    def halves(self, count, stage):
        return count % 32 == 0 and stage < self.stages - 1


def scratch_list(z):
    w, r, k = z.width, z.rows, z.keys
    v = pltpu.VMEM
    dma = pltpu.SemaphoreType.DMA
    n_units = len(z.units)
    if z.passes:
        extra = {"passed": v((2, 3, z.slots, z.pcol), BF16)}
    else:
        extra = {"hidden": v((z.ff_blocks, r, w), BF16)}
    return extra | {
        "row_io": v((3, r, w), BF16),
        "w_self": v((3, w, w), BF16),
        "w_cross": v((3, w, w), BF16),
        "w_mix": v((2, w, w), BF16),
        "w_exp": v((z.ff, w), BF16),
        "w_shr": v((z.ff, w), BF16),
        "packed": v((3, z.slots, z.pcol), BF16),
        "landed": v((3, z.slots, z.pcol), BF16),
        "back": v((3, z.slots, z.pcol), BF16),
        "place": v((z.parts, z.slots, r), BF16),
        "place_t": v((z.parts, r, z.slots), BF16),
        "compact": v((z.lanes_packed, z.parts, r, z.slots), BF16),
        "row_local": v((r, 128), F32),
        "bias": v((2, k, r), F32),
        "all_rows": v((2, k, w), BF16),
        "query": v((2, r, w), BF16),
        "key": v((2, k, w), BF16),
        "value": v((2, k, w), BF16),
        "score": v((k, 2 * r), F32),
        "lifted": v((2, z.pairs, k, 2 * r), BF16),
        "mixed_t": v((2, z.pairs, PAIR, r), BF16),
        "inverse": v((2, z.pairs, 8, 2 * r), F32),
        "mixed": v((2, r, w), BF16),
        "unit": v((3, r, w), F32),
        "spread": v((3, r, 128), F32),
        "stream": v((r, w), F32),
        "stream_low": v((2, r, w), BF16),
        "grad_in": v((r, w), BF16),
        "grad_q": v((r, w), BF16),
        "held": v((2, 2 * r, w), BF16),
        "held_y": v((2, r, w), BF16),
        "arrived": v((z.land_rows, w), BF16),
        "norm_acc": v((z.stages + 1, 8, w), F32),
        "norm_in": v((z.stages, 8, w), F32),
        "arrival": v((z.n_dp * z.n_seq * r // 128, 128), jnp.int32),
        "lengths": pltpu.SMEM((z.n_dp * z.group_sents,), jnp.int32),
        "flags": pltpu.SMEM((z.n_dp * z.group_sents,), jnp.int32),
        "gains": v((3, w), F32),
        "shifts": v((3, w), F32),
        "load_sem": dma((8,)),
        "small_sem": dma((5,)),
        "in_send": dma((3,)),
        "in_recv": dma((3, 4)),
        "back_send": dma((3,)),
        "back_recv": dma((3, 4)),
        "all_send": dma((2, 3, 4)),
        "all_recv": dma((2, 3, 4)),
        "part_send": dma((2, 3)),
        "part_recv": dma((2, 3)),
        "sum_send": dma((n_units, z.stages)),
        "sum_recv": dma((n_units, z.stages)),
        "sum_free": pltpu.SemaphoreType.REGULAR((n_units, z.stages)),
        "full_send": dma(()),
        "full_recv": dma((n_units, z.stages)),
        "norm_send": dma((z.stages,)),
        "norm_recv": dma((z.stages,)),
    }


INPUTS = (
    "arrival_hbm",
    "lengths_hbm",
    "flags_hbm",
    "tokens",
    "memory",
    "cotangent",
    "self_proj",
    "cross_proj",
    "mixers",
    "expander",
    "shrinker",
    "gains_hbm",
    "shifts_hbm",
)
OUTPUTS = ("layer_out", "token_grad", "memory_grad", "sums", "g_norm")


class Refs:
    pass


def layer_kernel(z, names, *refs):
    t = Refs()
    for name, ref in zip(names, refs):
        setattr(t, name, ref)
    group = lax.axis_index("dp")
    lane = lax.axis_index("seq")
    device = group * z.n_seq + lane
    rows, width, keys = z.rows, z.width, z.keys
    wide = lambda value: jnp.concatenate([value, value], axis=1)
    def partner(axis, bit):
        index = group if axis == "dp" else lane
        step = 1 << bit
        high = lax.rem(lax.div(index, step), 2)
        other = index + step * (1 - 2 * high)
        return high, other, ((other, lane) if axis == "dp" else (group, other))

    inputs = [
        pltpu.make_async_copy(source, t.row_io.at[k], t.load_sem.at[k])
        for k, source in enumerate((t.tokens, t.memory, t.cotangent))
    ]
    weights = [
        pltpu.make_async_copy(t.self_proj, t.w_self, t.load_sem.at[3]),
        pltpu.make_async_copy(t.mixers, t.w_mix, t.load_sem.at[4]),
        pltpu.make_async_copy(t.cross_proj, t.w_cross, t.load_sem.at[5]),
        pltpu.make_async_copy(t.shrinker, t.w_shr, t.load_sem.at[6]),
    ]
    for j in range(z.ff_blocks):
        weights.append(
            pltpu.make_async_copy(
                t.expander.at[:, block(j, width)], t.w_exp.at[block(j, width)], t.load_sem.at[7]
            )
        )
    small = [
        pltpu.make_async_copy(getattr(t, name + "_hbm"), getattr(t, name), t.small_sem.at[i])
        for i, name in enumerate(("arrival", "lengths", "flags", "gains", "shifts"))
    ]
    for copy in small[:1] + inputs + small[1:]:
        copy.start()

    barrier = pltpu.get_barrier_semaphore()

    def greet(j, carry):
        to = lax.rem(group + j, z.n_dp)
        pl.semaphore_signal(barrier, inc=1, device_id=(to, lane), device_id_type=MESH)
        return carry

    lax.fori_loop(1, z.n_dp, greet, 0)
    for j in range(1, z.n_seq):
        to = lax.rem(lane + j, z.n_seq)
        pl.semaphore_signal(barrier, inc=1, device_id=(group, to), device_id_type=MESH)

    shift = (z.n_seq * rows).bit_length() - 1
    small[0].wait()
    strips = rows // 128
    mine = t.arrival[pl.ds(device * strips, strips), :]
    mine = jnp.concatenate([mine[i : i + 1] for i in range(strips)], axis=1)
    target = lax.shift_right_logical(mine, shift)
    hit = jnp.where(iota((z.n_dp, rows), 0) == target, 1.0, 0.0)
    earlier = jnp.where(iota((rows, rows), 0) < iota((rows, rows), 1), 1.0, 0.0).astype(BF16)
    rank = jnp.sum(hit * nn(hit.astype(BF16), earlier), axis=0, keepdims=True)
    place = target * z.prow + rank.astype(jnp.int32)
    for part in range(z.parts):
        picks = jnp.where(iota((z.slots, rows), 0) == place + part * z.cap, 1.0, 0.0)
        t.place[part] = picks.astype(BF16)

    def pack(k, selector, source):
        total = None
        for part in range(z.parts):
            piece = source[:, part * z.pcol : (part + 1) * z.pcol]
            term = nn(selector[part], piece)
            total = term if total is None else total + term
        t.packed[k] = total.astype(BF16)

    quarter_size = z.n_dp // 4
    quarter, member = lax.div(group, quarter_size), lax.rem(group, quarter_size)
    quarter_rows = quarter_size * z.prow

    def crossed(i):
        high = lax.rem(lax.div(quarter, 2) + i // 2, 2)
        return 2 * high + lax.rem(lax.rem(quarter, 2) + i % 2, 2)

    def send_rows(k, landing, send_sem, recv_sem):
        own = block(group, z.prow)
        done = recv_sem.at[k, quarter]
        pltpu.make_async_copy(t.packed.at[k, own], landing.at[k, own], done).start()
        for i in (3, 2, 1, 0):
            first = crossed(i) * quarter_size

            def one(j, carry):
                to = first + lax.rem(member + j, quarter_size)
                pltpu.make_async_remote_copy(
                    src_ref=t.packed.at[k, block(to, z.prow)],
                    dst_ref=landing.at[k, own],
                    send_sem=send_sem.at[k],
                    recv_sem=done,
                    device_id=(to, lane),
                    device_id_type=MESH,
                ).start()
                return carry

            lax.fori_loop(1 if i == 0 else 0, quarter_size, one, 0)

    def wait_quarter(k, landing, recv_sem, i):
        which = crossed(i)
        at = landing.at[k, block(which, quarter_rows)]
        pltpu.make_async_copy(at, at, recv_sem.at[k, which]).wait()
        return block(which, quarter_rows)

    def wait_rows(k, landing, recv_sem):
        for i in range(4):
            wait_quarter(k, landing, recv_sem, i)

    def wait_sent(k, send_sem):
        others = pl.ds(0, (z.n_dp - 1) * z.prow)
        pltpu.make_async_copy(
            t.packed.at[k, others], t.packed.at[k, others], send_sem.at[k]
        ).wait()

    inputs[0].wait()
    pack(0, t.place, t.row_io[0])
    pl.semaphore_wait(barrier, z.n_dp - 1 + z.n_seq - 1)

    running, gathered, landed_count, exchanged, given = {}, {}, {}, set(), []

    def advance(name):
        try:
            next(running[name])
        except StopIteration:
            del running[name]

    def begin(name, task):
        next(task)
        running[name] = task

    def step(piece):
        if not z.planned:
            for name in list(running):
                advance(name)
            return
        for name in PLAN.get(piece, ()):
            if name in (X1, X2):
                start_exchange(1 + name - X1)
            elif name in running:
                advance(name)

    def finish(done=lambda: False):
        while running and not done():
            for name in list(running):
                advance(name)

    def start_exchange(k):
        if k in exchanged:
            return
        exchanged.add(k)
        send_rows(k, t.landed, t.in_send, t.in_recv)
        if z.passes and k < 2:
            for i in range(4):
                begin(P00 + 4 * k + i, pass_on(k, i))

    near_lane, near = partner("seq", 0)[1:]
    far_lane, far = partner("seq", 1)[1:]
    lanes = (lane, near_lane, far_lane, near_lane + (far_lane - lane))

    def passing(k, source, at, which, sem, to):
        return pltpu.make_async_remote_copy(
            src_ref=source.at[at],
            dst_ref=t.passed.at[k, which, at],
            send_sem=t.all_send.at[k, which, sem],
            recv_sem=t.all_recv.at[k, which, sem],
            device_id=to,
            device_id_type=MESH,
        )

    def pass_on(k, i):
        yield
        at = wait_quarter(k, t.landed, t.in_recv, i)
        landed_count[k] = landed_count.get(k, 0) + 1
        to_far = passing(k, t.landed.at[k], at, 0, i, far)
        to_far.start()
        yield
        to_far.wait()
        gathered[k, 0] = gathered.get((k, 0), 0) + 1
        if i % 2 == 1:
            half_at = block(lax.div(crossed(i), 2), 2 * quarter_rows)
            relay = passing(k, t.passed.at[k, 0], half_at, 2, i // 2, near)
            relay.start()
            yield
            relay.wait()
            gathered[k, 2] = gathered.get((k, 2), 0) + 2

    def pass_near(k):
        to_near = passing(k, t.landed.at[k], pl.ds(0, z.slots), 1, 0, near)
        to_near.start()
        yield
        to_near.wait()
        gathered[k, 1] = 4

    start_exchange(0)
    for copy in weights:
        copy.start()
    step(START)
    for k in (1, 2):
        inputs[k].wait()
        pack(k, t.place, t.row_io[k])
        step(PACK1 + k - 1)

    place_down = jnp.transpose(jnp.broadcast_to(place.astype(F32), (128, rows)))[:, 0:1].astype(jnp.int32)
    for part in range(z.parts):
        picks = jnp.where(iota((rows, z.slots), 1) == place_down + part * z.cap, 1.0, 0.0)
        t.place_t[part] = picks.astype(BF16)
    step(PLACE)
    n_all = z.n_dp * z.n_seq
    arrival = [t.arrival[pl.ds(i, n_all, stride=strips), :] for i in range(strips)]
    arrival = jnp.concatenate(arrival, axis=1)
    whose = lax.shift_right_logical(arrival, shift)
    ours = jnp.where(whose == group, 1.0, 0.0)
    local = (arrival - whose * (z.n_seq * rows)).astype(F32)
    within = nn(ours.astype(BF16), earlier)
    key_local = t.score.at[:, 0:128]
    rank_at = t.bias.at[0, 0:n_all, :]
    local_at = t.bias.at[0, n_all : 2 * n_all, :]
    rank_at[...] = jnp.where(ours > 0.5, within, -1.0)
    local_at[...] = local
    digits = t.lifted.at[1, 0]

    def slot_locals(index):
        chosen = rank_at[pl.ds(index, 1), :] == iota((z.prow, rows), 0).astype(F32)
        found = jnp.where(chosen, local_at[pl.ds(index, 1), :], 0.0)
        found = jnp.sum(found, axis=1, keepdims=True)
        high = jnp.floor(found * (1.0 / 32))
        pair = jnp.where(iota((z.prow, 128), 1) == 0, high, found - 32.0 * high)
        source, other = index // z.n_seq, index % z.n_seq
        digits[block(source, z.prow), block(other, 128)] = pair.astype(BF16)

    loop(n_all, slot_locals)
    step(SLOTS)
    down, across = iota((n_all, n_all), 0), iota((n_all, n_all), 1)
    same_lane = (down & (z.n_seq - 1)) == (across & (z.n_seq - 1))
    count_row = nt(jnp.ones((16, rows), BF16), ours.astype(BF16))
    after = jnp.where(same_lane & (down < across), 1.0, 0.0).astype(BF16)
    base_row = nn(count_row.astype(BF16), after)
    first_row = jnp.where(count_row > 0.5, base_row, -1024.0).astype(BF16)
    in_block = iota((1, z.slots), 1) & (z.prow - 1)
    from_source = lax.shift_right_logical(iota((n_all, z.slots), 1), z.prow.bit_length() - 1)
    for index in range(z.n_seq):
        wanted = from_source * z.n_seq + lanes[index]
        expand = jnp.where(iota((n_all, z.slots), 0) == wanted, 1.0, 0.0).astype(BF16)
        spot_row = nn(first_row, expand)[0:1, :].astype(jnp.int32)
        for part in range(z.parts):
            offset = in_block - part * z.cap
            spot = jnp.where((offset >= 0) & (offset < z.cap), spot_row + offset, -1)
            picks = jnp.where(spot == iota((rows, z.slots), 0), 1.0, 0.0).astype(BF16)
            if index < z.lanes_packed:
                t.compact[index, part] = picks
            if part == 0:
                found = nn(picks, digits[0 : z.slots, block(lanes[index], 128)])
                found = 32.0 * found[:, 0:1] + found[:, 1:2]
                key_local[block(lanes[index], rows), :] = jnp.broadcast_to(found, (rows, 128))
            if index == 0:
                spot_tall = jnp.broadcast_to(spot.astype(F32), (128, z.slots))
                spot_down = jnp.transpose(spot_tall)[:, 0:1].astype(jnp.int32)
                picks = jnp.where(spot_down == iota((z.slots, rows), 1), 1.0, 0.0)
                t.place[part] = picks.astype(BF16)
        step(LANE0 + index)

    def sentence_of(index):
        start, end, weight = jnp.zeros_like(index), jnp.zeros_like(index), jnp.zeros_like(index)
        edge = 0
        for j in range(z.group_sents):
            sentence = group * z.group_sents + j
            after = edge + t.lengths[sentence]
            low, high = jnp.float32(edge), after.astype(F32)
            share = jnp.where(t.flags[sentence] == 1, 1.0, SYNTH_WEIGHT)
            here = index >= low
            start = jnp.where(here, low, start)
            end = jnp.where(here, high, end)
            weight = jnp.where(here, share, weight)
            edge = after
        return start, end, weight

    for copy in small[1:]:
        copy.wait()
    own_local = key_local[block(lane, rows), :]
    t.row_local[...] = sentence_of(own_local)[2]
    query_local = jnp.transpose(own_local)[0:1, :]
    query_start, query_end, _ = sentence_of(query_local)

    def make_bias(j):
        here = key_local[block(j, rows), 0:1]
        late = here >= query_start
        t.bias[0, block(j, rows), :] = jnp.where(late & (here <= query_local), 0.0, SCORE_FILL)
        t.bias[1, block(j, rows), :] = jnp.where(late & (here < query_end), 0.0, SCORE_FILL)

    loop(z.n_seq, make_bias)
    step(BIAS)

    def unpack(selector, source):
        pieces = [nn(selector[part], source) for part in range(z.parts)]
        return pieces[0] if z.parts == 1 else jnp.concatenate(pieces, axis=1)

    def gather_seq(k):
        held = t.all_rows

        def copy(what, which, to):
            return pltpu.make_async_remote_copy(
                src_ref=held.at[k, what],
                dst_ref=held.at[k, what],
                send_sem=t.all_send.at[k, which, 0],
                recv_sem=t.all_recv.at[k, which, 0],
                device_id=to,
                device_id_type=MESH,
            )

        ours = block(lane, rows)
        to_far, to_near = copy(ours, 0, far), copy(ours, 1, near)
        relay = copy(block(far_lane, rows), 2, near)
        to_far.start()
        to_near.start()
        yield
        to_near.wait()
        to_far.wait()
        relay.start()
        gathered[k, 0] = gathered[k, 1] = 4
        yield
        relay.wait()
        gathered[k, 2] = 4

    def own_rows(k):
        if z.passes:
            finish(lambda: landed_count.get(k) == 4)
            begin(N0 + k, pass_near(k))
        else:
            wait_rows(k, t.landed, t.in_recv)
        t.all_rows[k, block(lane, rows), :] = unpack(t.compact.at[0], t.landed[k]).astype(BF16)
        if not z.passes:
            begin(N0 + k, gather_seq(k))

    def other_rows(k, which):
        finish(lambda: gathered.get((k, which)) == 4)
        index = (2, 1, 3)[which]
        if z.passes:
            found = unpack(t.compact.at[index], t.passed[k, which]).astype(BF16)
            t.all_rows[k, block(lanes[index], rows), :] = found
        return lanes[index]

    lanes_low = iota((rows, PAIR), 1) < HEAD
    tall_low = iota((PAIR, rows), 0) < HEAD
    none = jnp.zeros((), BF16)

    def stacked_queries(branch, p):
        pair = t.query[branch, :, block(p, PAIR)]
        return jnp.concatenate(
            [jnp.where(lanes_low, pair, none), jnp.where(lanes_low, none, pair)], axis=0
        )

    def stacked_tall(tall):
        return jnp.concatenate(
            [jnp.where(tall_low, tall, 0.0), jnp.where(tall_low, 0.0, tall)], axis=1
        )

    def split_pair(both):
        return jnp.concatenate([both[:HEAD, :rows], both[HEAD:, rows:]], axis=0)

    def attend_pair(branch, p):
        cols = block(p, PAIR)
        tall = jnp.transpose(t.query[branch, :, cols].astype(F32))
        stacked = stacked_tall(tall).astype(BF16)

        def scores(j, peak):
            at = block(j, rows)
            score = nn(t.key[branch, at, cols], stacked) + wide(t.bias[branch, at, :])
            t.score[at, :] = score
            return jnp.maximum(peak, jnp.max(score, axis=0, keepdims=True))

        peak = jnp.full((1, 2 * rows), -3e38, F32)
        for j in range(z.n_seq):
            peak = scores(j, peak)

        def lift(j, carry):
            total, mixed = carry
            at = block(j, rows)
            lifted = jnp.exp(t.score[at, :] - peak)
            low = lifted.astype(BF16)
            t.lifted[branch, p, at, :] = low
            return (
                total + jnp.sum(lifted, axis=0, keepdims=True),
                mixed + tn(t.value[branch, at, cols], low),
            )

        sums = (jnp.zeros((1, 2 * rows), F32), jnp.zeros((PAIR, 2 * rows), F32))
        for j in range(z.n_seq):
            sums = lift(j, sums)
        total, mixed = sums
        inverse = 1.0 / total
        t.inverse[branch, p] = jnp.broadcast_to(inverse, (8, 2 * rows))
        tall = split_pair(mixed * inverse)
        t.mixed_t[branch, p] = tall.astype(BF16)
        t.mixed[branch, :, cols] = jnp.transpose(tall).astype(BF16)

    def attend_back_pair(branch, p):
        cols = block(p, PAIR)
        stacked = stacked_queries(branch, p)
        inverse = t.inverse[branch, p, 0:1, :]
        tall = jnp.transpose(t.grad_in[:, cols].astype(F32))
        product = tall * t.mixed_t[branch, p].astype(F32)
        inner = inverse * jnp.concatenate(
            [
                jnp.sum(product[:HEAD], axis=0, keepdims=True),
                jnp.sum(product[HEAD:], axis=0, keepdims=True),
            ],
            axis=1,
        )
        both = stacked_tall(tall) * inverse
        both_down = jnp.transpose(both).astype(BF16)
        both = both.astype(BF16)

        def one(j, query_grad):
            at = block(j, rows)
            low = t.lifted[branch, p, at, :]
            prob_grad = nn(t.value[branch, at, cols], both)
            score_grad = (low.astype(F32) * (prob_grad - inner)).astype(BF16)
            t.w_shr[at, cols] = nn(score_grad, stacked).astype(BF16)
            t.w_shr[rows_at(keys + j * rows, rows), cols] = nn(low, both_down).astype(BF16)
            return query_grad + tn(t.key[branch, at, cols], score_grad)

        query_grad = jnp.zeros((PAIR, 2 * rows), F32)
        for j in range(z.n_seq):
            query_grad = one(j, query_grad)
        tall_grad = split_pair(query_grad) * HEAD ** (-0.5)
        t.grad_q[:, cols] = jnp.transpose(tall_grad).astype(BF16)

    def project_keys(branch, weight, j):
        at = block(j, rows)
        source = t.all_rows[branch, at, :]
        t.key[branch, at, :] = nn(source, weight[1]).astype(BF16)
        t.value[branch, at, :] = nn(source, weight[2]).astype(BF16)

    def norm_forward(values, i):
        center = values - jnp.sum(values, axis=-1, keepdims=True) * (1.0 / width)
        var = jnp.sum(center * center, axis=-1, keepdims=True) * (1.0 / width)
        scale = lax.rsqrt(var + EPSILON)
        unit = center * scale
        t.unit[i] = unit
        t.spread[i] = jnp.broadcast_to(scale, (rows, 128))
        return unit * t.gains[i : i + 1, :] + t.shifts[i : i + 1, :]

    def norm_backward(grad, i):
        unit = t.unit[i]
        t.norm_acc[0, i : i + 1, :] = jnp.sum(grad * unit, axis=0, keepdims=True)
        t.norm_acc[0, 3 + i : 4 + i, :] = jnp.sum(grad, axis=0, keepdims=True)
        scaled = grad * t.gains[i : i + 1, :]
        mean = jnp.sum(scaled, axis=-1, keepdims=True) * (1.0 / width)
        slope = jnp.sum(scaled * unit, axis=-1, keepdims=True) * (1.0 / width)
        return (scaled - mean - unit * slope) * t.spread[i, :, 0:1]

    def add_rows(offset, spot, count, cols):
        tile = next(s for s in (128, 96, 64, 48, 32, 16) if count % s == 0)

        def one(i):
            at = rows_at(offset + i * tile, tile)
            t.sums[at, cols] += t.arrived[rows_at(spot + i * tile, tile), cols]

        loop(count // tile, one)

    def sum_unit(name):
        unit, offset, count, first_col, n_cols, order = z.units[name]
        cols = pl.ds(first_col, n_cols)
        spot = z.land[name]
        halved, waiting = [], None
        for s, (axis, bit) in enumerate(order):
            high, _, to = partner(axis, bit)
            halving = z.halves(count, s)
            start = offset
            if halving:
                count //= 2
                keep, give = offset + high * count, offset + (1 - high) * count
                halved.append((s, high, to, axis, bit))
            else:
                keep = give = offset
            if waiting is not None:
                add_rows(give, waiting + (give - start), count, cols)
            copy = pltpu.make_async_remote_copy(
                src_ref=t.sums.at[rows_at(give, count), cols],
                dst_ref=t.arrived.at[rows_at(spot, count), cols],
                send_sem=t.sum_send.at[unit, s],
                recv_sem=t.sum_recv.at[unit, s],
                device_id=to,
                device_id_type=MESH,
            )
            copy.start()
            if waiting is not None and halving:
                add_rows(keep, waiting + (keep - start), count, cols)
            yield
            copy.wait()
            if halving:
                pl.semaphore_signal(
                    t.sum_free.at[unit, s], inc=1, device_id=to, device_id_type=MESH
                )
            offset = keep
            waiting = spot
            spot += count
        add_rows(offset, waiting, count, cols)
        for s, high, to, axis, bit in reversed(halved):
            held = t.sums.at[rows_at(offset, count), cols]
            copy = pltpu.make_async_remote_copy(
                src_ref=held,
                dst_ref=held,
                send_sem=t.full_send,
                recv_sem=t.full_recv.at[unit, s],
                device_id=to,
                device_id_type=MESH,
            )
            pl.semaphore_wait(t.sum_free.at[unit, s], 1)
            copy.start()
            given.append(count)
            yield
            copy.wait_recv()
            offset = offset - high * count
            count *= 2

    def sum_norms():
        for s, (axis, bit) in enumerate(z.order_a):
            _, _, to = partner(axis, bit)
            copy = pltpu.make_async_remote_copy(
                src_ref=t.norm_acc.at[s],
                dst_ref=t.norm_in.at[s],
                send_sem=t.norm_send.at[s],
                recv_sem=t.norm_recv.at[s],
                device_id=to,
                device_id_type=MESH,
            )
            copy.start()
            yield
            copy.wait()
            t.norm_acc[s + 1] = t.norm_acc[s] + t.norm_in[s]
        t.g_norm[...] = t.norm_acc[z.stages]

    def return_rows(k):
        wait_sent(k, t.in_send)
        pack(k, t.place, t.row_io[k])
        send_rows(k, t.back, t.back_send, t.back_recv)

    def return_part(branch, k, result):
        first = branch * keys
        cross_lane = lanes[3]

        def at(which):
            return rows_at(first + which * rows, rows)

        def copy(source, landing, which, to):
            return pltpu.make_async_remote_copy(
                src_ref=source,
                dst_ref=landing,
                send_sem=t.part_send.at[branch, which],
                recv_sem=t.part_recv.at[branch, which],
                device_id=to,
                device_id_type=MESH,
            )

        one = copy(t.w_exp.at[at(cross_lane)], t.held.at[branch, pl.ds(rows, rows)], 0, near)
        two = copy(t.w_exp.at[at(near_lane)], t.held.at[branch, pl.ds(0, rows)], 1, near)
        one.start()
        two.start()
        yield
        one.wait()
        t.w_exp[at(far_lane), :] = (
            t.w_exp[at(far_lane), :].astype(F32) + t.held[branch, rows:, :].astype(F32)
        ).astype(BF16)
        three = copy(t.w_exp.at[at(far_lane)], t.held_y.at[branch], 2, far)
        three.start()
        two.wait()
        yield
        three.wait()
        total = (
            t.w_exp[at(lane), :].astype(F32)
            + t.held[branch, :rows, :].astype(F32)
            + t.held_y[branch].astype(F32)
        )
        t.row_io[k] = total.astype(BF16)
        yield from bring_back(k, result)

    def bring_back(k, result):
        return_rows(k)
        yield
        wait_rows(k, t.back, t.back_recv)
        wait_sent(k, t.back_send)
        result[...] = unpack(t.place_t, t.back[k]).astype(BF16)

    def put_sum(name, j, value):
        first = z.units[name][1] + j * width
        t.sums[pl.ds(first, width), :] = value.astype(BF16)

    own = block(lane, rows)
    own_rows(0)
    start_exchange(1)
    step(OWN0)
    weights[0].wait()
    tokens = t.all_rows[0, own, :]
    t.query[0] = (nn(tokens, t.w_self[0]).astype(BF16).astype(F32) * HEAD ** (-0.5)).astype(BF16)
    project_keys(0, t.w_self, lane)
    step(Q0)
    for which, piece in ((1, NEAR0), (0, FAR0), (2, DIAG0)):
        project_keys(0, t.w_self, other_rows(0, which))
        step(piece)
    half = z.pairs // 2
    loop(half, functools.partial(attend_pair, 0))
    step(SATT0)
    loop(z.pairs - half, lambda p: attend_pair(0, half + p))
    step(SATT1)
    weights[1].wait()
    weights[2].wait()
    first = norm_forward(t.all_rows[0, own, :].astype(F32) + nn(t.mixed[0], t.w_mix[0]), 0)
    t.stream[...] = first
    t.stream_low[0] = first.astype(BF16)
    step(LN0)
    cross_query = nn(t.stream_low[0], t.w_cross[0]).astype(BF16)
    t.query[1] = (cross_query.astype(F32) * HEAD ** (-0.5)).astype(BF16)
    step(CQ)
    own_rows(1)
    start_exchange(2)
    step(OWN1)
    project_keys(1, t.w_cross, lane)
    step(KV1)
    for which, piece in ((1, NEAR1), (0, FAR1), (2, DIAG1)):
        project_keys(1, t.w_cross, other_rows(1, which))
        step(piece)
    loop(half, functools.partial(attend_pair, 1))
    step(CATT0)
    loop(z.pairs - half, lambda p: attend_pair(1, half + p))
    step(CATT1)

    second = norm_forward(t.stream[...] + nn(t.mixed[1], t.w_mix[1]), 1)
    t.stream[...] = second
    t.stream_low[1] = second.astype(BF16)
    for copy in weights[3:]:
        copy.wait()
    step(LN1)

    def hidden_at(j):
        if z.passes:
            return t.passed.at[0, j // 2, block(j % 2, rows), :]
        return t.hidden.at[j]

    def expand_block(j):
        pre = nn(t.stream_low[1], t.w_exp[block(j, width), :])
        gate = 0.5 + 0.5 * jnp.tanh(0.5 * pre)
        hidden = (pre * gate).astype(BF16)
        hidden_at(j)[...] = hidden
        t.score[block(j, rows), :] = gate * (1.0 + pre * (1.0 - gate))
        t.stream[...] += nn(hidden, t.w_shr[block(j, width), :])

    half = z.ff_blocks // 2
    for part in range(2):
        for j in range(half):
            expand_block(part * half + j)
        step(FFN0 + part)
    t.row_io[0] = norm_forward(t.stream[...], 2).astype(BF16)
    begin(OUT, bring_back(0, t.layer_out))
    step(LN2)

    wait_rows(2, t.landed, t.in_recv)
    grad = unpack(t.compact.at[0], t.landed[2]) * t.row_local[:, 0:1]
    t.stream[...] = norm_backward(grad, 2)
    t.grad_in[...] = t.stream[...].astype(BF16)
    step(COT)

    half = z.ff_blocks // 2
    for part, name in enumerate((SHR0, SHR1)):
        for j in range(half):
            put_sum(name, j, tn(hidden_at(part * half + j)[...], t.grad_in[...]))
        begin(name, sum_unit(name))
        step(FB0 + part)

    def expand_back(part, j, name):
        cols = block(part * half + j, width)
        pre_grad = nt(t.grad_in[...], t.w_shr[cols, :]) * t.score[block(part * half + j, rows), :]
        low = pre_grad.astype(BF16)
        put_sum(name, j, tn(t.stream_low[1], low))
        t.stream[...] += nt(low, t.w_exp[cols, :])

    for part, name in enumerate((EXP0, EXP1)):
        for j in range(half):
            expand_back(part, j, name)
        begin(name, sum_unit(name))
        step(FB2 + part)
    t.stream[...] = norm_backward(t.stream[...], 1)
    low = t.stream[...].astype(BF16)
    put_sum(CROSS_Q, 0, tn(t.mixed[1], low))
    t.grad_in[...] = nt(low, t.w_mix[1]).astype(BF16)
    step(LN1B)

    def row_part(branch, weight):
        def one(j):
            at = block(j, rows)
            total = nt(t.w_shr[at, :], weight[1]) + nt(
                t.w_shr[rows_at(keys + j * rows, rows), :], weight[2]
            )
            t.w_exp[rows_at(branch * keys + j * rows, rows), :] = total.astype(BF16)

        loop(z.n_seq, one)

    def key_sums(branch, which):
        first = which * keys

        def one(j, total):
            return total + tn(
                t.all_rows[branch, block(j, rows), :], t.w_shr[rows_at(first + j * rows, rows), :]
            )

        return lax.fori_loop(0, z.n_seq, one, jnp.zeros((width, width), F32))

    def attention_back(branch, weight, first, source, k, result):
        q_sum, kv_sum = ((SELF_Q, SELF_KV), (CROSS_Q, CROSS_KV))[branch]
        half = z.pairs // 2
        for part in range(2):
            loop(half, lambda p: attend_back_pair(branch, part * half + p))
            step(first + part)
        row_part(branch, weight)
        if branch == 0:
            t.w_exp[own, :] = (
                t.w_exp[own, :].astype(F32) + t.stream[...] + nt(t.grad_q[...], weight[0])
            ).astype(BF16)
        begin(RET0 + branch, return_part(branch, k, result))
        step(first + 2)
        put_sum(q_sum, 1, tn(source[...], t.grad_q[...]))
        begin(q_sum, sum_unit(q_sum))
        step(first + 3)
        put_sum(kv_sum, 0, key_sums(branch, 0))
        step(first + 4)
        put_sum(kv_sum, 1, key_sums(branch, 1))
        begin(kv_sum, sum_unit(kv_sum))
        step(first + 5)

    attention_back(1, t.w_cross, CROSS_B0, t.stream_low.at[0], 2, t.memory_grad)
    t.stream[...] = norm_backward(t.stream[...] + nt(t.grad_q[...], t.w_cross[0]), 0)
    t.norm_acc[0, 6:8, :] = jnp.zeros((2, width), F32)
    begin(NORM, sum_norms())
    step(LN0B)
    low = t.stream[...].astype(BF16)
    put_sum(SELF_Q, 0, tn(t.mixed[0], low))
    t.grad_in[...] = nt(low, t.w_mix[0]).astype(BF16)
    step(MIX0)
    attention_back(0, t.w_self, SELF_B0, t.all_rows.at[0, own], 1, t.token_grad)
    finish()
    total = t.sums.at[pl.ds(0, sum(given)), :]
    pltpu.make_async_copy(total, total, t.full_send).wait()


def finish_kernel(z, *refs):
    w = z.width
    sums, rows, norms = refs[0], refs[1:4], refs[4]
    g_self, g_cross, g_mix, g_exp, g_shr = refs[5:10]
    done, gains, shifts, full, out_sem, row_sem = refs[10:13], *refs[13:]
    copies = [pltpu.make_async_copy(a, b, row_sem.at[i]) for i, (a, b) in enumerate(zip(rows, done))]
    for copy in copies:
        copy.start()
    gains[...] = norms[0:3, :]
    shifts[...] = norms[3:6, :]
    pieces = []
    half = z.ff_blocks // 2
    for j in range(z.ff_blocks):
        for name, result in (((SHR0, SHR1)[j // half], g_shr), ((EXP0, EXP1)[j // half], g_exp)):
            spot = (block(j, w), slice(None)) if result is g_shr else (slice(None), block(j, w))
            pieces.append((z.units[name][1] + (j % half) * w, result.at[spot]))
    for j, (name, result) in enumerate(((SELF_Q, g_self), (CROSS_Q, g_cross))):
        first = z.units[name][1]
        pieces.append((first, g_mix.at[j]))
        pieces += [(first + (1 + i) * w, result.at[i]) for i in range(3)]

    def widen(first, i):
        def one(c):
            at = rows_at(first + c * 64, 64)
            full[i, block(c, 64), :] = sums[at, :].astype(F32)

        loop(w // 64, one)

    for i, (first, result) in enumerate(pieces):
        widen(first, i)
        copy = pltpu.make_async_copy(full.at[i], result, out_sem.at[i])
        copy.start()
        copies.append(copy)
    for copy in copies:
        copy.wait()


def body(
    z,
    tokens,
    memory,
    cotangent,
    arrival_order,
    lengths,
    real_flag,
    self_proj,
    cross_proj,
    mixers,
    expander,
    shrinker,
    norm_gains,
    norm_shifts,
):
    scratch = scratch_list(z)
    names = INPUTS + OUTPUTS + tuple(scratch)
    w = z.width
    anywhere = pl.BlockSpec(memory_space=pl.ANY)
    vmem = pl.BlockSpec(memory_space=pltpu.VMEM)
    results = pl.pallas_call(
        functools.partial(layer_kernel, z, names),
        out_shape=(pltpu.VMEM((z.rows, w), BF16),) * 3
        + (pltpu.VMEM((z.sum_rows, w), BF16), pltpu.VMEM((8, w), F32)),
        in_specs=[anywhere] * 13,
        out_specs=[vmem] * 5,
        scratch_shapes=list(scratch.values()),
        compiler_params=pltpu.CompilerParams(
            collective_id=0, has_side_effects=True, vmem_limit_bytes=LAYER_VMEM
        ),
        name="layer",
    )(
        arrival_order.reshape(-1, 128),
        lengths,
        real_flag,
        tokens,
        memory,
        cotangent,
        self_proj,
        cross_proj,
        mixers,
        expander,
        shrinker,
        norm_gains,
        norm_shifts,
    )
    *row_results, sums, norms = results
    n_blocks = z.sum_rows // w
    wide = [(3, w, w), (3, w, w), (2, w, w), (w, z.ff), (z.ff, w)]
    done = pl.pallas_call(
        functools.partial(finish_kernel, z),
        out_shape=tuple(jax.ShapeDtypeStruct(shape, F32) for shape in wide)
        + (jax.ShapeDtypeStruct((z.rows, w), BF16),) * 3
        + (jax.ShapeDtypeStruct((3, w), F32),) * 2,
        in_specs=[vmem] * 5,
        out_specs=[anywhere] * 8 + [vmem] * 2,
        scratch_shapes=[
            pltpu.VMEM((n_blocks, w, w), F32),
            pltpu.SemaphoreType.DMA((n_blocks,)),
            pltpu.SemaphoreType.DMA((3,)),
        ],
        compiler_params=pltpu.CompilerParams(vmem_limit_bytes=FINISH_VMEM),
        name="widen",
    )(sums, *row_results, norms)
    return (*done[5:8], *done[:5], *done[8:])


def solution(mesh):
    n_dp, n_seq = mesh.shape["dp"], mesh.shape["seq"]

    def whole(*arrays):
        tokens, lengths, expander = arrays[0], arrays[4], arrays[9]
        z = Sizes(
            n_dp,
            n_seq,
            tokens.shape[0] // (n_dp * n_seq),
            tokens.shape[1],
            expander.shape[1],
            lengths.shape[0],
        )
        split = P(("dp", "seq"), None)
        return jax.shard_map(
            functools.partial(body, z),
            mesh=mesh,
            in_specs=(split,) * 3 + (P(),) * 10,
            out_specs=(split,) * 3 + (P(),) * 7,
            check_vma=False,
        )(*arrays)

    return whole
```
